256 devices in a mesh: seq: 32 (over z_hi, y, core), head: 8 (over z_lo, x).
Axes of the slice: x: 4, y: 4, z: 8 (z_hi: 4, z_lo: 2; z = z_hi * 2 + z_lo), core: 2. Of those that a mesh axis runs over, the one named last changes fastest.
Arguments:
- queries: bfloat16 [16384, 2048], P('seq', 'head'), may hold values from -25 to 25
- key_frames: bfloat16 [16384, 2048], P('seq', 'head'), may hold values from -4 to 4
- value_frames: bfloat16 [16384, 2048], P('seq', 'head'), may hold values from -6 to 6
- out_weight: bfloat16 [2048, 2048], P('head'), may hold values from -0.125 to 0.125
- out_grad: bfloat16 [16384, 2048], P('seq', 'head'), may hold values from -6 to 6
- near_window: int32 [32], replicated, may hold values from 1 to 2, as said below
- mid_start: int32 [32], replicated, may hold values from 0 to 31, as said below
Outputs:
- layer_out: bfloat16 [16384, 2048], P('seq', 'head')
- query_grad: bfloat16 [16384, 2048], P('seq', 'head')
- key_grad: bfloat16 [16384, 2048], P('seq', 'head')
- value_grad: bfloat16 [16384, 2048], P('seq', 'head')
- weight_grad: float32 [2048, 2048], P('head', 'seq')
The draws below stay inside these ranges and needn't reach their ends.
Inputs may be any that keep to these rules, and one draw needn't show every extreme that they name: mid_start[b] lies between 0 and b; the last block's value is 31. near_window is 1 on block 0 and 2 on every other block.
All inputs are finite; a program needn't handle non-finite values.
Results may differ from the reference program's by a relative error of at most 0.028.
Values may be sent and summed in bfloat16 or wider, within the bound.
No kernel may reach another device: no remote copies, remote signals or barrier semaphores. Data moves between devices by JAX's collectives and lax.ppermute only.
A program may use at most 128 MiB of HBM per device.

```python
import math
import jax
import jax.numpy as jnp
from jax import lax

HEADS = 16
HEAD_DIM = 128
WIDTH = 2048
BLOCK = 512
POOL_MID = 8
POOL_FAR = 64
FRAMES_DEV = 512
FRAMES = 16384
BLOCKS = 32


def shared_keys(key):
    full_shape = (FRAMES, HEADS * HEAD_DIM)
    normal_part = jnp.clip(jax.random.normal(jax.random.fold_in(key, 11), full_shape, jnp.float32), -4.0, 4.0)
    return normal_part


def draw_key_frames(key, part):
    normal_part = shared_keys(key)
    return normal_part.astype(jnp.bfloat16)


def draw_queries(key, part):
    key = jax.random.fold_in(key, 2)
    full_shape = (FRAMES, HEADS * HEAD_DIM)
    return jnp.clip(jax.random.normal(key, full_shape, jnp.float32), -4.0, 4.0).astype(jnp.bfloat16)


def draw_mid_start(key, part):
    key = jax.random.fold_in(key, 3)
    block_ids = jnp.arange(BLOCKS, dtype=jnp.int32)
    drawn = jax.random.randint(key, (BLOCKS,), 0, block_ids + 1, dtype=jnp.int32)
    return jnp.where(block_ids == BLOCKS - 1, BLOCKS - 1, drawn).astype(jnp.int32)


def draw_near_window(key, part):
    key = jax.random.fold_in(key, 4)
    block_ids = jnp.arange(BLOCKS, dtype=jnp.int32)
    drawn = jax.random.randint(key, (BLOCKS,), 1, 3, dtype=jnp.int32)
    run_start = block_ids % (FRAMES_DEV // BLOCK) == 0
    forced = jnp.where(run_start, 2, drawn)
    return jnp.where(block_ids == 0, 1, forced).astype(jnp.int32)


def shard_levels(stream_key, shape, shards, smallest, top_value):
    level, own = 1.0, jax.random.fold_in(stream_key, 6)
    for position, blocks in shards:
        draws = jnp.exp(jax.random.uniform(jax.random.fold_in(own, position), (blocks,), jnp.float32, smallest / len(shards), top_value / len(shards)))
        level = level * jnp.repeat(draws, shape[position] // blocks).reshape([-1 if axis == position else 1 for axis in range(len(shape))])
    return level


def centred(stream_key, extent, scale, bound, pieces=(), held_as=jnp.bfloat16):
    loudness = shard_levels(stream_key, extent, pieces, -0.22, 0.18) if pieces else 1.0
    values = jax.random.normal(stream_key, extent, jnp.float32) * scale * loudness
    return jnp.minimum(jnp.maximum(values, -bound), bound).astype(held_as)


def setup_inputs(seed: int = 0) -> dict:
    streams_of = jax.random.split(jax.random.key(seed), 8)
    queries = draw_queries(jax.random.fold_in(streams_of[7], 71), 0)
    key_frames = draw_key_frames(jax.random.fold_in(streams_of[7], 71), 0)
    value_frames = centred(streams_of[2], (FRAMES, WIDTH), 1.0, 6.0, ((0, 32), (1, 8)))
    out_weight = centred(streams_of[3], (WIDTH, WIDTH), WIDTH ** -0.5, 0.125, ((0, 8),))
    out_grad = centred(streams_of[4], (FRAMES, WIDTH), 1.0, 6.0, ((0, 32), (1, 8)))
    near_window = draw_near_window(jax.random.fold_in(streams_of[7], 71), 0)
    mid_start = draw_mid_start(jax.random.fold_in(streams_of[7], 71), 0)
    return {"queries": queries, "key_frames": key_frames, "value_frames": value_frames, "out_weight": out_weight, "out_grad": out_grad, "near_window": near_window, "mid_start": mid_start}


NEGATIVE = -1.0e30


def pooled_mean(frames, factor):
    row_count, columns = frames.shape
    grouped = frames.astype(jnp.float32).reshape(row_count // factor, factor, columns)
    return jnp.mean(grouped, axis=1).astype(jnp.bfloat16)


def spread_rows(pooled, factor):
    row_count, columns = pooled.shape
    return jnp.broadcast_to(pooled[:, None, :], (row_count, factor, columns)).reshape(row_count * factor, columns)


def windows(frames, before, blocks):
    joined = jnp.concatenate([before, frames], axis=0).reshape(blocks + 1, BLOCK, HEAD_DIM)
    return jnp.concatenate([joined[:-1], joined[1:]], axis=1)


def row_bounds(begin, factor):
    edge_rows = begin * (BLOCK // factor)
    return jnp.broadcast_to(edge_rows[:, None], (begin.shape[0], BLOCK)).reshape(-1)


def head_levels(query_rows, key_head, value_head, near_begin, mid_begin):
    frames = query_rows.shape[0]
    blocks = frames // BLOCK
    scaling = HEAD_DIM ** -0.5
    block_ids = jnp.arange(blocks, dtype=jnp.int32)
    zero_block = jnp.zeros((BLOCK, HEAD_DIM), query_rows.dtype)
    key_win = windows(key_head, zero_block, blocks)
    value_win = windows(value_head, zero_block, blocks)
    query_blocks = query_rows.reshape(blocks, BLOCK, HEAD_DIM)
    query_pos = jnp.arange(BLOCK, dtype=jnp.int32)
    key_pos = jnp.arange(2 * BLOCK, dtype=jnp.int32) - BLOCK
    lowest = ((near_begin - block_ids) * BLOCK)[:, None, None]
    near_allowed = (key_pos[None, None, :] >= lowest) & (key_pos[None, None, :] <= query_pos[None, :, None])
    near_scores = jnp.einsum("nqd,nkd->nqk", query_blocks.astype(jnp.float32), key_win.astype(jnp.float32)) * scaling
    near_scores = jnp.where(near_allowed, near_scores, NEGATIVE)
    key_mid = pooled_mean(key_head, POOL_MID)
    value_mid = pooled_mean(value_head, POOL_MID)
    key_far = pooled_mean(key_head, POOL_FAR)
    value_far = pooled_mean(value_head, POOL_FAR)
    mid_index = jnp.arange(key_mid.shape[0], dtype=jnp.int32)
    mid_allowed = (mid_index[None, :] >= row_bounds(mid_begin, POOL_MID)[:, None]) & (mid_index[None, :] < row_bounds(near_begin, POOL_MID)[:, None])
    mid_scores = jnp.dot(query_rows, key_mid.T, preferred_element_type=jnp.float32) * scaling + math.log(POOL_MID)
    mid_scores = jnp.where(mid_allowed, mid_scores, NEGATIVE)
    far_index = jnp.arange(key_far.shape[0], dtype=jnp.int32)
    far_allowed = far_index[None, :] < row_bounds(mid_begin, POOL_FAR)[:, None]
    far_scores = jnp.dot(query_rows, key_far.T, preferred_element_type=jnp.float32) * scaling + math.log(POOL_FAR)
    far_scores = jnp.where(far_allowed, far_scores, NEGATIVE)
    row_top = jnp.maximum(jnp.max(near_scores, axis=-1).reshape(frames), jnp.maximum(jnp.max(mid_scores, axis=-1), jnp.max(far_scores, axis=-1)))
    near_exp = jnp.exp(near_scores - row_top.reshape(blocks, BLOCK)[..., None])
    mid_exp = jnp.exp(mid_scores - row_top[:, None])
    far_exp = jnp.exp(far_scores - row_top[:, None])
    totals = jnp.sum(near_exp, axis=-1).reshape(frames) + jnp.sum(mid_exp, axis=-1) + jnp.sum(far_exp, axis=-1)
    near_weights = near_exp / totals.reshape(blocks, BLOCK)[..., None]
    mid_weights = mid_exp / totals[:, None]
    far_weights = far_exp / totals[:, None]
    return (near_weights, mid_weights, far_weights, key_win, value_win, query_blocks, key_mid, value_mid, key_far, value_far)


def head_forward(query_rows, key_head, value_head, near_begin, mid_begin):
    frames = query_rows.shape[0]
    levels = head_levels(query_rows, key_head, value_head, near_begin, mid_begin)
    near_weights, mid_weights, far_weights, key_win, value_win = levels[0], levels[1], levels[2], levels[3], levels[4]
    value_mid, value_far = levels[7], levels[9]
    near_w16 = lax.optimization_barrier(near_weights.astype(jnp.bfloat16))
    near_out = jnp.einsum("nqk,nkd->nqd", near_w16.astype(jnp.float32), value_win.astype(jnp.float32)).reshape(frames, HEAD_DIM)
    mid_out = jnp.dot(mid_weights.astype(jnp.bfloat16), value_mid, preferred_element_type=jnp.float32)
    far_out = jnp.dot(far_weights.astype(jnp.bfloat16), value_far, preferred_element_type=jnp.float32)
    return (near_out + mid_out + far_out).astype(jnp.bfloat16)


def head_backward(query_rows, key_head, value_head, attention_head, grad_head, near_begin, mid_begin):
    frames = query_rows.shape[0]
    blocks = frames // BLOCK
    scaling = HEAD_DIM ** -0.5
    levels = head_levels(query_rows, key_head, value_head, near_begin, mid_begin)
    near_weights, mid_weights, far_weights, key_win, value_win, query_blocks = levels[0], levels[1], levels[2], levels[3], levels[4], levels[5]
    key_mid, value_mid, key_far, value_far = levels[6], levels[7], levels[8], levels[9]
    near_w16 = lax.optimization_barrier(near_weights.astype(jnp.bfloat16))
    mid_w16 = mid_weights.astype(jnp.bfloat16)
    far_w16 = far_weights.astype(jnp.bfloat16)
    row_delta = jnp.sum(grad_head.astype(jnp.float32) * attention_head.astype(jnp.float32), axis=-1)
    grad_blocks = grad_head.reshape(blocks, BLOCK, HEAD_DIM)
    near_dp = jnp.einsum("nqd,nkd->nqk", grad_blocks.astype(jnp.float32), value_win.astype(jnp.float32))
    near_ds = lax.optimization_barrier((near_weights * (near_dp - row_delta.reshape(blocks, BLOCK)[..., None])).astype(jnp.bfloat16))
    mid_dp = jnp.dot(grad_head, value_mid.T, preferred_element_type=jnp.float32)
    mid_ds = (mid_weights * (mid_dp - row_delta[:, None])).astype(jnp.bfloat16)
    far_dp = jnp.dot(grad_head, value_far.T, preferred_element_type=jnp.float32)
    far_ds = (far_weights * (far_dp - row_delta[:, None])).astype(jnp.bfloat16)
    query_sum = jnp.einsum("nqk,nkd->nqd", near_ds.astype(jnp.float32), key_win.astype(jnp.float32)).reshape(frames, HEAD_DIM)
    query_sum = query_sum + jnp.dot(mid_ds, key_mid, preferred_element_type=jnp.float32) + jnp.dot(far_ds, key_far, preferred_element_type=jnp.float32)
    query_grad = (scaling * query_sum).astype(jnp.bfloat16)
    key_win_grad = jnp.einsum("nqk,nqd->nkd", near_ds.astype(jnp.float32), query_blocks.astype(jnp.float32)) * scaling
    value_win_grad = jnp.einsum("nqk,nqd->nkd", near_w16.astype(jnp.float32), grad_blocks.astype(jnp.float32))
    last_zero = jnp.zeros((1, BLOCK, HEAD_DIM), jnp.float32)
    key_near = key_win_grad[:, BLOCK:] + jnp.concatenate([key_win_grad[1:, :BLOCK], last_zero], axis=0)
    value_near = value_win_grad[:, BLOCK:] + jnp.concatenate([value_win_grad[1:, :BLOCK], last_zero], axis=0)
    mid_key_grad = jnp.dot(mid_ds.T, query_rows, preferred_element_type=jnp.float32) * scaling
    mid_value_grad = jnp.dot(mid_w16.T, grad_head, preferred_element_type=jnp.float32)
    far_key_grad = jnp.dot(far_ds.T, query_rows, preferred_element_type=jnp.float32) * scaling
    far_value_grad = jnp.dot(far_w16.T, grad_head, preferred_element_type=jnp.float32)
    key_total = key_near.reshape(frames, HEAD_DIM) + spread_rows(mid_key_grad, POOL_MID) / POOL_MID + spread_rows(far_key_grad, POOL_FAR) / POOL_FAR
    value_total = value_near.reshape(frames, HEAD_DIM) + spread_rows(mid_value_grad, POOL_MID) / POOL_MID + spread_rows(far_value_grad, POOL_FAR) / POOL_FAR
    return (query_grad, key_total.astype(jnp.bfloat16), value_total.astype(jnp.bfloat16))


def reference(queries, key_frames, value_frames, out_weight, out_grad, near_window, mid_start):
    frames = queries.shape[0]
    block_ids = jnp.arange(frames // BLOCK, dtype=jnp.int32)
    near_begin = jnp.maximum(block_ids + 1 - near_window, 0)
    mid_begin = jnp.minimum(mid_start, near_begin)

    def by_head(matrix):
        return matrix.reshape(frames, HEADS, HEAD_DIM).transpose(1, 0, 2)

    def by_rows(stacked):
        return stacked.transpose(1, 0, 2).reshape(frames, HEADS * HEAD_DIM)

    def forward_one(head_items):
        return head_forward(head_items[0], head_items[1], head_items[2], near_begin, mid_begin)

    def backward_one(head_items):
        return head_backward(head_items[0], head_items[1], head_items[2], head_items[3], head_items[4], near_begin, mid_begin)

    query_heads = by_head(queries)
    key_heads = by_head(key_frames)
    value_heads = by_head(value_frames)
    attention_heads = lax.map(forward_one, (query_heads, key_heads, value_heads))
    attention = by_rows(attention_heads)
    layer_out = jnp.dot(attention, out_weight, preferred_element_type=jnp.float32).astype(jnp.bfloat16)
    attention_grad = jnp.dot(out_grad, out_weight.T, preferred_element_type=jnp.float32).astype(jnp.bfloat16)
    weight_grad = jnp.dot(attention.T, out_grad, preferred_element_type=jnp.float32)
    grads = lax.map(backward_one, (query_heads, key_heads, value_heads, attention_heads, by_head(attention_grad)))
    return (layer_out, by_rows(grads[0]), by_rows(grads[1]), by_rows(grads[2]), weight_grad)
```

```python
import math

import jax
import jax.numpy as jnp
from jax import lax
from jax.experimental import pallas as pl
from jax.experimental.pallas import tpu as pltpu
from jax.sharding import PartitionSpec as P

HEAD_DIM = 128
BLOCK = 512
POOL_MID = 8
POOL_FAR = 64
MIDS = BLOCK // POOL_MID
HEADS_DEV = 2
COLS = HEADS_DEV * HEAD_DIM
HEAD_DEVS = 8
Z, Y, C = 4, 4, 2
CHUNK = Z * MIDS
CHUNKS = Y * C
FAR_KEYS = CHUNKS * CHUNK

NEGATIVE = -1e30
SCALING = HEAD_DIM ** (-0.5)
LOG2E = math.log2(math.e)
SCORE_SCALE = SCALING * LOG2E
MID_BIAS = math.log2(POOL_MID)

bf16 = jnp.bfloat16
f32 = jnp.float32


def shifted(value, dz=0, dy=0, dc=0):
    pairs = []
    for z in range(Z):
        for y in range(Y):
            for c in range(C):
                target = (((z + dz) % Z) * Y + (y + dy) % Y) * C + (c + dc) % C
                pairs.append(((z * Y + y) * C + c, target))
    return lax.ppermute(value, "seq", pairs)


def passed_along(value, steps):
    count = Z * Y * C
    initial, last = (max(0, -steps), min(count, count - steps))
    return lax.ppermute(value, "seq", [(source, source + steps) for source in range(initial, last)])


def shape(*dims, dtype=bf16):
    return jax.ShapeDtypeStruct(dims, dtype)


def call(kernel, outs, scratch=(), smem=0, flops=0, count=0):
    def run(*args):
        moved = sum(a.size * a.dtype.itemsize for a in (*args, *outs))
        return pl.pallas_call(
            kernel,
            out_shape=list(outs),
            in_specs=[pl.BlockSpec(memory_space=pltpu.SMEM)] * smem
            + [pl.BlockSpec(memory_space=pltpu.VMEM)] * (len(args) - smem),
            out_specs=[pl.BlockSpec(memory_space=pltpu.VMEM)] * len(outs),
            scratch_shapes=list(scratch),
            cost_estimate=pl.CostEstimate(flops=flops, bytes_accessed=moved, transcendentals=count),
            compiler_params=pltpu.CompilerParams(vmem_limit_bytes=44 * 1024 * 1024),
        )(*args)

    return run


def place():
    s = lax.axis_index("seq")
    return s, s >> 3, (s >> 1) & 3, s & 1


def block_of(z, y, c, group, dz):
    core = (c + (group >> 2)) & 1
    return ((z - dz) & 3) * 8 + ((y - group) & 3) * 2 + core


def dot(a, b, da, db):
    return lax.dot_general(a, b, (((da,), (db,)), ((), ())), preferred_element_type=f32)


def total(*refs):
    s = refs[0][...].astype(f32)
    for r in refs[1:]:
        s = s + r[...].astype(f32)
    return s


def pool_kernel(k_ref, v_ref, out_ref):
    row = lax.broadcasted_iota(jnp.int32, (MIDS, BLOCK), 0)
    col = lax.broadcasted_iota(jnp.int32, (MIDS, BLOCK), 1)
    mean = jnp.where(row == col // POOL_MID, 1.0 / POOL_MID, 0.0).astype(bf16)
    out_ref[:, :COLS] = dot(mean, k_ref[...], 1, 0).astype(bf16)
    out_ref[:, COLS:] = dot(mean, v_ref[...], 1, 0).astype(bf16)


def own_mask(first_key, queries_from, keys, queries):
    key = lax.broadcasted_iota(jnp.int32, (keys, queries), 0) + first_key
    query = lax.broadcasted_iota(jnp.int32, (keys, queries), 1) + queries_from
    return key <= query


def forward_kernel(nw_ref, ms_ref, q_ref, k_ref, v_ref, pk_ref, pv_ref, *refs):
    mids = refs[:CHUNKS]
    w_ref, att_ref, lse_ref, kv_ref, out_ref, s_ref, bias_ref = refs[CHUNKS:]
    s, z, y, c = place()
    near_begin = jnp.maximum(s + 1 - nw_ref[s], 0)
    mid_begin = jnp.minimum(ms_ref[s], near_begin)
    row = lax.broadcasted_iota(jnp.int32, (CHUNK, CHUNK), 0)
    col = lax.broadcasted_iota(jnp.int32, (CHUNK, CHUNK), 1)
    same = jnp.where(row == col, 1.0, 0.0)
    mean = jnp.where(row // POOL_MID == col // POOL_MID, 1.0 / POOL_MID, 0.0)
    for g in range(CHUNKS):
        picks = []
        for dz in range(Z):
            b = block_of(z, y, c, g, dz)
            bias_ref[g * Z + dz] = jnp.where(b < near_begin, MID_BIAS, NEGATIVE)
            far = jnp.where(b < mid_begin, 1.0, 0.0)
            rows = slice(dz * MIDS, (dz + 1) * MIDS)
            picks.append(same[rows] + far * (mean[rows] - same[rows]))
        pick = jnp.concatenate(picks, axis=0).astype(bf16)
        kv_ref[g * CHUNK : (g + 1) * CHUNK, :] = dot(pick, mids[g][...], 1, 0).astype(bf16)
    prev_bias = jnp.where(near_begin < s, 0.0, NEGATIVE)
    half = BLOCK // 2
    for h in range(HEADS_DEV):
        cols = slice(h * HEAD_DIM, (h + 1) * HEAD_DIM)
        vcols = slice(COLS + h * HEAD_DIM, COLS + (h + 1) * HEAD_DIM)
        q = q_ref[:, cols]
        sc = dot(k_ref[:half, cols], q, 1, 1) * SCORE_SCALE
        sc = jnp.where(own_mask(0, 0, half, BLOCK), sc, NEGATIVE)
        s_ref[FAR_KEYS : FAR_KEYS + half, :] = sc
        top = jnp.max(sc, axis=0, keepdims=True)
        sc = dot(k_ref[half:, cols], q, 1, 1) * SCORE_SCALE
        sc = jnp.where(own_mask(half, 0, half, BLOCK), sc, NEGATIVE)
        s_ref[FAR_KEYS + half : FAR_KEYS + BLOCK, :] = sc
        top = jnp.maximum(top, jnp.max(sc, axis=0, keepdims=True))
        for part in range(2):
            keys = slice(part * half, (part + 1) * half)
            sc = dot(pk_ref[keys, cols], q, 1, 1) * SCORE_SCALE + prev_bias
            s_ref[FAR_KEYS + BLOCK + part * half : FAR_KEYS + BLOCK + (part + 1) * half, :] = sc
            top = jnp.maximum(top, jnp.max(sc, axis=0, keepdims=True))

        def scores(g, top):
            rows = pl.ds(pl.multiple_of(g * CHUNK, CHUNK), CHUNK)
            sc = dot(kv_ref[rows, cols], q, 1, 1) * SCORE_SCALE
            sc = jnp.concatenate(
                [sc[d * MIDS : (d + 1) * MIDS] + bias_ref[g * Z + d] for d in range(Z)], axis=0
            )
            s_ref[rows, :] = sc
            return jnp.maximum(top, jnp.max(sc, axis=0, keepdims=True))

        top = lax.fori_loop(0, CHUNKS, scores, top, unroll=2)

        def step(score, values):
            e = jnp.exp2(score - top)
            return jnp.sum(e, axis=0, keepdims=True), dot(values, e.astype(bf16), 0, 0)

        def gather(g, carry):
            rows = pl.ds(pl.multiple_of(g * CHUNK, CHUNK), CHUNK)
            a, b = step(s_ref[rows, :], kv_ref[rows, vcols])
            return carry[0] + a, carry[1] + b

        sums, out = lax.fori_loop(
            0,
            CHUNKS,
            gather,
            (jnp.zeros((1, BLOCK), f32), jnp.zeros((HEAD_DIM, BLOCK), f32)),
            unroll=2,
        )
        for part in range(4):
            values = (v_ref, pv_ref)[part // 2][(part % 2) * half : (part % 2 + 1) * half, cols]
            a, b = step(
                s_ref[FAR_KEYS + part * half : FAR_KEYS + (part + 1) * half, :], values
            )
            sums, out = sums + a, out + b
        att_ref[:, cols] = (out / sums).T.astype(bf16)
        lse_ref[h : h + 1, :] = top + jnp.log2(sums)
    for i in range(HEAD_DEVS):
        out_ref[i * BLOCK : (i + 1) * BLOCK, :] = dot(
            att_ref[...], w_ref[:, i * COLS : (i + 1) * COLS], 1, 0
        ).astype(bf16)


def project_kernel(att_ref, grad_ref, w_ref, dout_ref, own_ref, other_ref):
    s, z, y, c = place()
    acc = jnp.zeros((BLOCK, COLS), f32)
    for i in range(HEAD_DEVS):
        grad = grad_ref[i * BLOCK : (i + 1) * BLOCK, :]
        acc = acc + dot(grad, w_ref[:, i * COLS : (i + 1) * COLS], 1, 1)
        term = dot(grad, att_ref[...], 0, 0).astype(bf16)
        for part in range(COLS // MIDS):
            block = i * (COLS // MIDS) + part
            bz, by, bc = block >> 3, (block >> 1) & 3, block & 1
            row = pl.multiple_of((((y - by) & 3) * Z + ((z - bz) & 3)) * MIDS, MIDS)
            piece = term[part * MIDS : (part + 1) * MIDS]

            @pl.when(c == bc)
            def _():
                own_ref[pl.ds(row, MIDS), :] = piece

            @pl.when(c != bc)
            def _():
                other_ref[pl.ds(row, MIDS), :] = piece

    dout_ref[...] = acc.astype(bf16)


def backward_kernel(
    nw_ref, ms_ref, q_ref, k_ref, v_ref, pk_ref, pv_ref, kv_ref, att_ref, lse_ref, do_ref,
    dq_ref, own_near_ref, rim_ref, own_ref, other_ref, bias_ref,
):
    s, z, y, c = place()
    near_begin = jnp.maximum(s + 1 - nw_ref[s], 0)
    for g in range(CHUNKS):
        for dz in range(Z):
            bias_ref[g * Z + dz] = jnp.where(
                block_of(z, y, c, g, dz) < near_begin, MID_BIAS, NEGATIVE
            )
    prev_bias = jnp.where(near_begin < s, 0.0, NEGATIVE)
    half = BLOCK // 2
    for h in range(HEADS_DEV):
        cols = slice(h * HEAD_DIM, (h + 1) * HEAD_DIM)
        vcols = slice(COLS + h * HEAD_DIM, COLS + (h + 1) * HEAD_DIM)
        q, do = q_ref[:, cols], do_ref[:, cols]
        lse = lse_ref[h : h + 1, :]
        delta = jnp.sum(
            (do.astype(f32) * att_ref[:, cols].astype(f32)).T, axis=0, keepdims=True
        )

        def step(keys, values, bias):
            w = jnp.exp2(bias(dot(keys, q, 1, 1) * SCORE_SCALE) - lse)
            ds = (w * (dot(values, do, 1, 1) - delta)).astype(bf16)
            dv = dot(w.astype(bf16), do, 1, 0)
            dk = dot(ds, q, 1, 0) * SCALING
            return dk, dv, dot(keys, ds, 0, 0)

        def middle(out, first, acc):
            def body(i, acc):
                g = i + first
                rows = pl.ds(pl.multiple_of(g * CHUNK, CHUNK), CHUNK)

                def bias(sc):
                    return jnp.concatenate(
                        [sc[d * MIDS : (d + 1) * MIDS] + bias_ref[g * Z + d] for d in range(Z)],
                        axis=0,
                    )

                dk, dv, dq = step(kv_ref[rows, cols], kv_ref[rows, vcols], bias)
                target = pl.ds(pl.multiple_of(i * CHUNK, CHUNK), CHUNK)
                out[target, cols] = dk.astype(bf16)
                out[target, vcols] = dv.astype(bf16)
                return acc + dq

            return lax.fori_loop(0, CHUNKS // 2, body, acc, unroll=2)

        acc = jnp.zeros((HEAD_DIM, BLOCK), f32)
        acc = middle(other_ref, CHUNKS // 2, acc)
        acc = middle(own_ref, 0, acc)
        for part in range(2):
            rows = slice(part * half, (part + 1) * half)
            dk, dv, dq = step(pk_ref[rows, cols], pv_ref[rows, cols], lambda sc: sc + prev_bias)
            rim_ref[rows, cols] = dk.astype(bf16)
            rim_ref[rows, vcols] = dv.astype(bf16)
            acc = acc + dq
            dk, dv, dq = step(
                k_ref[rows, cols],
                v_ref[rows, cols],
                lambda sc: jnp.where(own_mask(part * half, 0, half, BLOCK), sc, NEGATIVE),
            )
            own_near_ref[rows, cols] = dk
            own_near_ref[rows, vcols] = dv
            acc = acc + dq
        dq_ref[:, cols] = (acc * SCALING).T.astype(bf16)


def core_sum_kernel(own_ref, got_ref, *outs):
    for i, out in enumerate(outs):
        rows = slice(i * CHUNK, (i + 1) * CHUNK)
        out[...] = (own_ref[rows].astype(f32) + got_ref[rows].astype(f32)).astype(bf16)


def y_sum_kernel(a, b, c, d, *outs):
    for i, out in enumerate(outs):
        rows = pl.ds(i * MIDS, MIDS)
        out[...] = total(a.at[rows], b.at[rows], c.at[rows], d.at[rows]).astype(bf16)


def weight_kernel(a, b, c, d, out_ref):
    out_ref[...] = total(a, b, c, d).T


def key_value_kernel(near_ref, rim_ref, a, b, c, d, key_ref, value_ref):
    mid = total(a, b, c, d) * (1.0 / POOL_MID)
    spread = jnp.broadcast_to(mid[:, None, :], (MIDS, POOL_MID, 2 * COLS)).reshape(BLOCK, 2 * COLS)
    grad = near_ref[...] + rim_ref[...].astype(f32) + spread
    key_ref[...] = grad[:, :COLS].astype(bf16)
    value_ref[...] = grad[:, COLS:].astype(bf16)


def staged_sum(own, other):
    width = own.shape[1]
    got = shifted(other, dc=1)
    parts = call(core_sum_kernel, [shape(CHUNK, width)] * Y)(own, got)
    parts = [parts[0]] + [shifted(parts[i], dy=-i) for i in range(1, Y)]
    parts = call(y_sum_kernel, [shape(MIDS, width)] * Z)(*parts)
    return [parts[0]] + [shifted(parts[i], dz=-i) for i in range(1, Z)]


def on_device(queries, key_frames, value_frames, out_weight, out_grad, near_window, mid_start):
    grad_rows = lax.all_gather(out_grad, "head", axis=0, tiled=True)
    (mid,) = call(pool_kernel, [shape(MIDS, 2 * COLS)])(key_frames, value_frames)
    zs = [mid] + [shifted(mid, dz=i) for i in range(1, Z)]
    prev_keys, prev_values = passed_along(key_frames, 1), passed_along(value_frames, 1)
    run = jnp.concatenate(zs, axis=0)
    own_core = [run] + [shifted(run, dy=i) for i in range(1, Y)]
    other_core = [shifted(v, dc=1) for v in own_core]

    attention, lse, kv, projected = call(
        forward_kernel,
        [
            shape(BLOCK, COLS),
            shape(HEADS_DEV, BLOCK, dtype=f32),
            shape(FAR_KEYS, 2 * COLS),
            shape(HEAD_DEVS * BLOCK, COLS),
        ],
        scratch=[
            pltpu.VMEM((FAR_KEYS + 2 * BLOCK, BLOCK), f32),
            pltpu.SMEM((CHUNKS * Z,), f32),
        ],
        smem=2,
        flops=4 * 2 * BLOCK * 3072 * 128,
        count=2 * BLOCK * 3072,
    )(
        near_window, mid_start, queries, key_frames, value_frames, prev_keys, prev_values,
        *own_core, *other_core, out_weight,
    )
    layer_out = lax.psum_scatter(projected, "head", scatter_dimension=0, tiled=True)

    attention_grad, weight_own, weight_other = call(
        project_kernel,
        [shape(BLOCK, COLS), shape(FAR_KEYS // 2, COLS), shape(FAR_KEYS // 2, COLS)],
        flops=4 * BLOCK * 2048 * COLS,
    )(attention, grad_rows, out_weight)
    weight_parts = staged_sum(weight_own, weight_other)

    query_grad, near_grad, rim, mid_own, mid_other = call(
        backward_kernel,
        [
            shape(BLOCK, COLS),
            shape(BLOCK, 2 * COLS, dtype=f32),
            shape(BLOCK, 2 * COLS),
            shape(FAR_KEYS // 2, 2 * COLS),
            shape(FAR_KEYS // 2, 2 * COLS),
        ],
        scratch=[pltpu.SMEM((CHUNKS * Z,), f32)],
        smem=2,
        flops=10 * 2 * BLOCK * 3072 * 128,
        count=2 * BLOCK * 3072,
    )(
        near_window, mid_start, queries, key_frames, value_frames, prev_keys, prev_values,
        kv, attention, lse, attention_grad,
    )
    rim_got = passed_along(rim, -1)
    mid_parts = staged_sum(mid_own, mid_other)
    (weight_grad,) = call(weight_kernel, [shape(COLS, MIDS, dtype=f32)])(*weight_parts)
    key_grad, value_grad = call(key_value_kernel, [shape(BLOCK, COLS), shape(BLOCK, COLS)])(
        near_grad, rim_got, *mid_parts
    )
    return layer_out, query_grad, key_grad, value_grad, weight_grad


def solution(mesh):
    return jax.shard_map(
        on_device,
        mesh=mesh,
        in_specs=(
            P("seq", "head"),
            P("seq", "head"),
            P("seq", "head"),
            P("head", None),
            P("seq", "head"),
            P(),
            P(),
        ),
        out_specs=(
            P("seq", "head"),
            P("seq", "head"),
            P("seq", "head"),
            P("seq", "head"),
            P("head", "seq"),
        ),
        check_vma=False,
    )
```

```python
import math

import jax
import jax.numpy as jnp
from jax import lax
from jax.experimental import pallas as pl
from jax.experimental.pallas import tpu as pltpu
from jax.sharding import PartitionSpec as P

HEAD_DIM = 128
BLOCK = 512
POOL_MID = 8
MIDS = BLOCK // POOL_MID
HEADS_DEV = 2
COLS = HEADS_DEV * HEAD_DIM
Z, Y, C = 4, 4, 2
ZL, X = 2, 4
CHUNK = Z * MIDS
CHUNKS = Y * C
FAR_KEYS = CHUNKS * CHUNK
HALF = BLOCK // 2
SUM_COLS = 3 * COLS

NEGATIVE = -1e30
SCALING = HEAD_DIM ** (-0.5)
SCORE_SCALE = SCALING * math.log2(math.e)
MID_BIAS = math.log2(POOL_MID)

bf16 = jnp.bfloat16
f32 = jnp.float32


def along_seq(value, dz=0, dy=0, dc=0):
    pairs = []
    for z in range(Z):
        for y in range(Y):
            for c in range(C):
                target = (((z + dz) % Z) * Y + (y + dy) % Y) * C + (c + dc) % C
                pairs.append(((z * Y + y) * C + c, target))
    return lax.ppermute(value, "seq", pairs)


def along_head(value, dz=0, dx=0):
    pairs = []
    for z in range(ZL):
        for x in range(X):
            pairs.append((z * X + x, ((z + dz) % ZL) * X + (x + dx) % X))
    return lax.ppermute(value, "head", pairs)


def along_z(value, step):
    return along_seq(value, dz=step)


def along_y(value, step):
    return along_seq(value, dy=step)


def along_x(value, step):
    return along_head(value, dx=step)


def passed_along(value, steps):
    count = Z * Y * C
    initial, last = (max(0, -steps), min(count, count - steps))
    return lax.ppermute(value, "seq", [(source, source + steps) for source in range(initial, last)])


def shape(*dims, dtype=bf16):
    return jax.ShapeDtypeStruct(dims, dtype)


def call(kernel, outs, scratch=(), far=0, flops=0, count=0):
    def run(*args):
        moved = sum(a.size * a.dtype.itemsize for a in (*args, *outs))
        return pl.pallas_call(
            kernel,
            out_shape=list(outs),
            in_specs=[pl.BlockSpec(memory_space=pl.ANY)] * far
            + [pl.BlockSpec(memory_space=pltpu.VMEM)] * (len(args) - far),
            out_specs=[pl.BlockSpec(memory_space=pltpu.VMEM)] * len(outs),
            scratch_shapes=list(scratch),
            cost_estimate=pl.CostEstimate(flops=flops, bytes_accessed=moved, transcendentals=count),
            compiler_params=pltpu.CompilerParams(vmem_limit_bytes=40 * 1024 * 1024),
        )(*args)

    return run


def place():
    s = lax.axis_index("seq")
    return s, s >> 3, (s >> 1) & 3, s & 1


def block_of(z, y, c, group, dz):
    core = (c + (group >> 2)) & 1
    return ((z - dz) & 3) * 8 + ((y - group) & 3) * 2 + core


def dot(a, b, da, db):
    return lax.dot_general(a, b, (((da,), (db,)), ((), ())), preferred_element_type=f32)


def wide(ref, rows):
    return ref[rows].astype(f32)


def emit(chunk, outs):
    behind, ahead, late_behind, late_ahead, own = outs
    h = chunk(0).shape[0] // 2
    behind[:h], behind[h:] = chunk(1)[h:], chunk(2)[:h]
    ahead[:h], ahead[h:] = chunk(3)[:h], chunk(2)[h:]
    late_behind[...], late_ahead[...] = chunk(1)[:h], chunk(3)[h:]
    own[...] = chunk(0)


def ring_shapes(rows, width):
    h = rows // 2
    return [shape(rows, width)] * 2 + [shape(h, width)] * 2 + [shape(rows, width)]


def turn_kernel(late_behind, late_ahead, got_behind, got_ahead, out_behind, out_ahead):
    h = late_behind.shape[0]
    rest, all_rows = slice(h, 2 * h), slice(0, h)
    out_behind[...] = (wide(late_behind, all_rows) + wide(got_behind, rest)).astype(bf16)
    out_ahead[...] = (wide(late_ahead, all_rows) + wide(got_ahead, rest)).astype(bf16)


def ring(parts, along):
    behind, ahead, late_behind, late_ahead, own = parts
    got_behind, got_ahead = along(behind, -1), along(ahead, 1)
    turned = [shape(*late_behind.shape)] * 2
    out_behind, out_ahead = call(turn_kernel, turned)(
        late_behind, late_ahead, got_behind, got_ahead
    )
    return own, got_behind, got_ahead, along(out_behind, -1), along(out_ahead, 1)


def halves(own, got_behind, got_ahead, last_behind, last_ahead):
    h = last_behind.shape[0]
    first, rest = slice(0, h), slice(h, 2 * h)
    a = wide(own, first) + wide(got_ahead, first) + wide(last_behind, first)
    b = wide(own, rest) + wide(got_behind, first) + wide(last_ahead, first)
    return a, b


def pool_kernel(k_hbm, v_hbm, kv_ref, mid_ref, sems):
    copies = [
        pltpu.make_async_copy(k_hbm, kv_ref.at[:, :COLS], sems.at[0]),
        pltpu.make_async_copy(v_hbm, kv_ref.at[:, COLS:], sems.at[1]),
    ]
    for copy in copies:
        copy.start()
    row = lax.broadcasted_iota(jnp.int32, (MIDS, BLOCK), 0)
    col = lax.broadcasted_iota(jnp.int32, (MIDS, BLOCK), 1)
    mean = jnp.where(row == col // POOL_MID, 1.0 / POOL_MID, 0.0).astype(bf16)
    for copy in copies:
        copy.wait()
    mid_ref[...] = dot(mean, kv_ref[...], 1, 0).astype(bf16)


def own_mask(first_key):
    key = lax.broadcasted_iota(jnp.int32, (HALF, BLOCK), 0) + first_key
    query = lax.broadcasted_iota(jnp.int32, (HALF, BLOCK), 1)
    return key <= query


def chunk_bias(bias_ref, g, scores):
    return jnp.concatenate(
        [scores[d * MIDS : (d + 1) * MIDS] + bias_ref[g * Z + d] for d in range(Z)], axis=0
    )


def chunk_rows(g):
    return pl.ds(pl.multiple_of(g * CHUNK, CHUNK), CHUNK)


def head_cols(h):
    return slice(h * HEAD_DIM, (h + 1) * HEAD_DIM), slice(
        COLS + h * HEAD_DIM, COLS + (h + 1) * HEAD_DIM
    )


def weight_cols(zl, x, dx, dz):
    device = ((zl + dz) & 1) * X + ((x - dx) & 3)
    return device, pl.ds(pl.multiple_of(device * COLS, COLS), COLS)


def forward_kernel(
    nw_hbm, ms_hbm, q_hbm, w_hbm, kv_ref, pkv_ref, *refs
):
    mids = refs[:CHUNKS]
    att_ref, lse_ref, far_ref = refs[CHUNKS : CHUNKS + 3]
    outs = refs[CHUNKS + 3 : CHUNKS + 8]
    q_ref, w_ref, s_ref, nw_ref, ms_ref, bias_ref, sems = refs[CHUNKS + 8 :]
    copies = [
        pltpu.make_async_copy(a, b, sems.at[i])
        for i, (a, b) in enumerate(
            ((q_hbm, q_ref), (nw_hbm, nw_ref), (ms_hbm, ms_ref), (w_hbm, w_ref))
        )
    ]
    for copy in copies:
        copy.start()
    s, z, y, c = place()
    row = lax.broadcasted_iota(jnp.int32, (CHUNK, CHUNK), 0)
    col = lax.broadcasted_iota(jnp.int32, (CHUNK, CHUNK), 1)
    same = jnp.where(row == col, 1.0, 0.0)
    mean = jnp.where(row // POOL_MID == col // POOL_MID, 1.0 / POOL_MID, 0.0)
    for copy in copies[:3]:
        copy.wait()
    near_begin = jnp.maximum(s + 1 - nw_ref[s], 0)
    mid_begin = jnp.minimum(ms_ref[s], near_begin)
    for g in range(CHUNKS):
        picks = []
        for dz in range(Z):
            b = block_of(z, y, c, g, dz)
            bias_ref[g * Z + dz] = jnp.where(b < near_begin, MID_BIAS, NEGATIVE)
            far = jnp.where(b < mid_begin, 1.0, 0.0)
            rows = slice(dz * MIDS, (dz + 1) * MIDS)
            picks.append(same[rows] + far * (mean[rows] - same[rows]))
        pick = jnp.concatenate(picks, axis=0).astype(bf16)
        far_ref[g * CHUNK : (g + 1) * CHUNK, :] = dot(pick, mids[g][...], 1, 0).astype(bf16)
    prev_bias = jnp.where(near_begin < s, 0.0, NEGATIVE)
    for h in range(HEADS_DEV):
        cols, vcols = head_cols(h)
        q = q_ref[:, cols]
        top = jnp.full((1, BLOCK), NEGATIVE, f32)
        for part in range(4):
            keys = (kv_ref, pkv_ref)[part // 2][(part % 2) * HALF : (part % 2 + 1) * HALF, cols]
            sc = dot(keys, q, 1, 1) * SCORE_SCALE
            if part < 2:
                sc = jnp.where(own_mask(part * HALF), sc, NEGATIVE)
            else:
                sc = sc + prev_bias
            s_ref[FAR_KEYS + part * HALF : FAR_KEYS + (part + 1) * HALF, :] = sc
            top = jnp.maximum(top, jnp.max(sc, axis=0, keepdims=True))

        def scores(g, top):
            rows = chunk_rows(g)
            sc = chunk_bias(bias_ref, g, dot(far_ref[rows, cols], q, 1, 1) * SCORE_SCALE)
            s_ref[rows, :] = sc
            return jnp.maximum(top, jnp.max(sc, axis=0, keepdims=True))

        top = lax.fori_loop(0, CHUNKS, scores, top, unroll=2)

        def step(score, values):
            e = jnp.exp2(score - top)
            return jnp.sum(e, axis=0, keepdims=True), dot(values, e.astype(bf16), 0, 0)

        def gather(g, carry):
            a, b = step(s_ref[chunk_rows(g), :], far_ref[chunk_rows(g), vcols])
            return carry[0] + a, carry[1] + b

        start = (jnp.zeros((1, BLOCK), f32), jnp.zeros((HEAD_DIM, BLOCK), f32))
        sums, out = lax.fori_loop(0, CHUNKS, gather, start, unroll=2)
        for part in range(4):
            values = (kv_ref, pkv_ref)[part // 2][(part % 2) * HALF : (part % 2 + 1) * HALF, vcols]
            rows = slice(FAR_KEYS + part * HALF, FAR_KEYS + (part + 1) * HALF)
            a, b = step(s_ref[rows, :], values)
            sums, out = sums + a, out + b
        att_ref[:, cols] = (out / sums).T.astype(bf16)
        lse_ref[h : h + 1, :] = top + jnp.log2(sums)
    copies[3].wait()
    me = lax.axis_index("head")
    zl, x = me >> 2, me & 3

    def projected(dx, dz):
        columns = weight_cols(zl, x, dx, dz)[1]
        return dot(att_ref[...], w_ref[:, columns], 1, 0).astype(bf16)

    behind, ahead, late_behind, late_ahead, own = outs
    behind[:BLOCK], behind[BLOCK:] = projected(1, 1), projected(2, 0)
    ahead[:BLOCK], ahead[BLOCK:] = projected(3, 0), projected(2, 1)
    late_behind[...], late_ahead[...] = projected(1, 0), projected(3, 1)
    own[:BLOCK], own[BLOCK:] = projected(0, 0), projected(0, 1)


def prepare(nw_hbm, nw_ref, sem):
    copy = pltpu.make_async_copy(nw_hbm, nw_ref, sem)
    copy.start()
    return copy


def step(keys, values, q, do, lse, delta, bias):
    w = jnp.exp2(bias(dot(keys, q, 1, 1) * SCORE_SCALE) - lse)
    ds = (w * (dot(values, do, 1, 1) - delta)).astype(bf16)
    dv = dot(w.astype(bf16), do, 1, 0)
    dk = dot(ds, q, 1, 0) * SCALING
    return dk, dv, dot(keys, ds, 0, 0)


def far_part(first, refs, bias_ref, near_begin, out_ref, dq_in, dq_out):
    q_ref, far_ref, lse_ref, do_ref, delta_ref = refs
    s, z, y, c = place()
    for g in range(first, first + Y):
        for dz in range(Z):
            b = block_of(z, y, c, g, dz)
            bias_ref[g * Z + dz] = jnp.where(b < near_begin, MID_BIAS, NEGATIVE)
    for h in range(HEADS_DEV):
        cols, vcols = head_cols(h)
        q, do = q_ref[:, cols], do_ref[:, cols]
        lse, delta = lse_ref[h : h + 1, :], delta_ref[h : h + 1, :]

        def body(i, acc):
            g = i + first
            rows = chunk_rows(g)
            dk, dv, dq = step(
                far_ref[rows, cols], far_ref[rows, vcols], q, do, lse, delta,
                lambda sc: chunk_bias(bias_ref, g, sc),
            )
            out_ref[chunk_rows(i), cols] = dk.astype(bf16)
            out_ref[chunk_rows(i), vcols] = dv.astype(bf16)
            return acc + dq

        acc = jnp.zeros((HEAD_DIM, BLOCK), f32) if dq_in is None else dq_in[cols, :]
        dq_out[cols, :] = lax.fori_loop(0, Y, body, acc, unroll=2)


def other_kernel(nw_hbm, q_hbm, w_hbm, far_ref, att_ref, lse_ref, *refs):
    grads = refs[: ZL * X]
    do_ref, delta_ref, dq_ref, weight_ref, out_ref, q_ref, w_ref, nw_ref, bias_ref, sems = refs[ZL * X :]
    copies = [
        pltpu.make_async_copy(a, b, sems.at[i])
        for i, (a, b) in enumerate(((w_hbm, w_ref), (nw_hbm, nw_ref), (q_hbm, q_ref)))
    ]
    for copy in copies:
        copy.start()
    s, z, y, c = place()
    me = lax.axis_index("head")
    zl, x = me >> 2, me & 3
    copies[0].wait()
    acc = jnp.zeros((BLOCK, COLS), f32)
    for i in range(ZL * X):
        device, columns = weight_cols(zl, x, i % X, i // X)
        grad = grads[i][...]
        acc = acc + dot(grad, w_ref[:, columns], 1, 1)
        term = dot(grad, att_ref[...], 0, 0).astype(bf16)
        for part in range(COLS // MIDS):
            block = device * (COLS // MIDS) + part
            bz, by = block >> 3, (block >> 1) & 3
            row = pl.multiple_of((((y - by) & 3) * Z + ((z - bz) & 3)) * MIDS, MIDS)
            piece = term[part * MIDS : (part + 1) * MIDS]

            @pl.when(c == part % 2)
            def _():
                weight_ref[pl.ds(row, MIDS), :] = piece

            @pl.when(c != part % 2)
            def _():
                out_ref[pl.ds(row, MIDS), 2 * COLS :] = piece

    do_ref[...] = acc.astype(bf16)
    for h in range(HEADS_DEV):
        cols, _ = head_cols(h)
        product = do_ref[:, cols].astype(f32) * att_ref[:, cols].astype(f32)
        delta_ref[h : h + 1, :] = jnp.sum(product.T, axis=0, keepdims=True)
    copies[1].wait()
    copies[2].wait()
    near_begin = jnp.maximum(s + 1 - nw_ref[s], 0)
    parts = (q_ref, far_ref, lse_ref, do_ref, delta_ref)
    far_part(Y, parts, bias_ref, near_begin, out_ref, None, dq_ref)


def own_kernel(
    nw_hbm, q_hbm, far_ref, lse_ref, do_ref, delta_ref, dq_in, weight_ref, out_ref, dq_ref,
    q_ref, nw_ref, bias_ref, sems,
):
    copies = [
        pltpu.make_async_copy(a, b, sems.at[i])
        for i, (a, b) in enumerate(((q_hbm, q_ref), (nw_hbm, nw_ref)))
    ]
    for copy in copies:
        copy.start()
    out_ref[:, 2 * COLS :] = weight_ref[...]
    for copy in copies:
        copy.wait()
    s = place()[0]
    near_begin = jnp.maximum(s + 1 - nw_ref[s], 0)
    parts = (q_ref, far_ref, lse_ref, do_ref, delta_ref)
    far_part(0, parts, bias_ref, near_begin, out_ref, dq_in, dq_ref)


def near_kernel(
    nw_hbm, q_hbm, kv_ref, pkv_ref, lse_ref, do_ref, delta_ref, dq_in, dq_ref, near_ref, rim_ref,
    q_ref, nw_ref, sems,
):
    copies = [
        pltpu.make_async_copy(a, b, sems.at[i])
        for i, (a, b) in enumerate(((q_hbm, q_ref), (nw_hbm, nw_ref)))
    ]
    for copy in copies:
        copy.start()
    for copy in copies:
        copy.wait()
    s = place()[0]
    near_begin = jnp.maximum(s + 1 - nw_ref[s], 0)
    prev_bias = jnp.where(near_begin < s, 0.0, NEGATIVE)
    for h in range(HEADS_DEV):
        cols, vcols = head_cols(h)
        q, do = q_ref[:, cols], do_ref[:, cols]
        lse, delta = lse_ref[h : h + 1, :], delta_ref[h : h + 1, :]
        acc = dq_in[cols, :]
        for part in range(2):
            rows = slice(part * HALF, (part + 1) * HALF)
            dk, dv, dq = step(
                pkv_ref[rows, cols], pkv_ref[rows, vcols], q, do, lse, delta,
                lambda sc: sc + prev_bias,
            )
            rim_ref[rows, cols] = dk.astype(bf16)
            rim_ref[rows, vcols] = dv.astype(bf16)
            acc = acc + dq
            dk, dv, dq = step(
                kv_ref[rows, cols], kv_ref[rows, vcols], q, do, lse, delta,
                lambda sc: jnp.where(own_mask(part * HALF), sc, NEGATIVE),
            )
            near_ref[rows, cols] = dk
            near_ref[rows, vcols] = dv
            acc = acc + dq
        dq_ref[:, cols] = (acc * SCALING).T.astype(bf16)


def core_kernel(own_ref, got_ref, *outs):
    def chunk(i):
        rows = slice(i * CHUNK, (i + 1) * CHUNK)
        return (wide(own_ref, rows) + wide(got_ref, rows)).astype(bf16)

    emit(chunk, outs)


def y_kernel(*refs):
    a, b = halves(*refs[:5])
    both = [h[i * MIDS : (i + 1) * MIDS].astype(bf16) for h in (a, b) for i in range(2)]
    emit(lambda i: both[i], refs[5:])


def x_kernel(own, got_behind, got_ahead, last_behind, last_ahead, keep_ref, pass_ref):
    a, b = halves(own, got_behind, got_ahead, last_behind, last_ahead)
    keep_ref[...] = a
    pass_ref[...] = b.astype(bf16)


def pair_kernel(keep_ref, got_ref, out_ref):
    out_ref[...] = (keep_ref[...] + got_ref[...].astype(f32)).astype(bf16)


def last_kernel(own, got_behind, got_ahead, last_behind, last_ahead, near_ref, rim_ref, key_ref, value_ref, weight_ref):
    total = jnp.concatenate(
        halves(own, got_behind, got_ahead, last_behind, last_ahead), axis=0
    )
    weight_ref[...] = total[:, 2 * COLS :]
    mid = total[:, : 2 * COLS] * (1.0 / POOL_MID)
    spread = jnp.broadcast_to(mid[:, None, :], (MIDS, POOL_MID, 2 * COLS)).reshape(BLOCK, 2 * COLS)
    grad = near_ref[...] + rim_ref[...].astype(f32) + spread
    key_ref[...] = grad[:, :COLS].astype(bf16)
    value_ref[...] = grad[:, COLS:].astype(bf16)


def on_device(queries, key_frames, value_frames, out_weight, out_grad, near_window, mid_start):
    dma = pltpu.SemaphoreType.DMA
    smem_window = pltpu.SMEM((Z * Y * C,), jnp.int32)
    smem_bias = pltpu.SMEM((CHUNKS * Z,), f32)
    vmem_q = pltpu.VMEM((BLOCK, COLS), bf16)
    vmem_w = pltpu.VMEM((COLS, ZL * X * COLS), bf16)
    pair_flops = 2 * HEADS_DEV * BLOCK * HEAD_DIM

    kv, mid = call(
        pool_kernel, [shape(BLOCK, 2 * COLS), shape(MIDS, 2 * COLS)], [dma((2,))], far=2
    )(key_frames, value_frames)
    run = jnp.concatenate([mid] + [along_z(mid, i) for i in range(1, Z)], axis=0)
    prev_kv = passed_along(kv, 1)
    ahead, behind = along_y(run, 1), along_y(run, -1)
    beyond = jnp.concatenate(
        [along_y(ahead[: CHUNK // 2], 1), along_y(behind[CHUNK // 2 :], -1)], axis=0
    )
    own_core = [run, ahead, beyond, behind]
    other_core = [along_seq(v, dc=1) for v in own_core]

    mine = out_grad
    pair = along_head(out_grad, dz=1)
    ahead_g, behind_g = along_x(mine, 1), along_x(mine, -1)
    ahead_p, behind_p = along_x(pair, 1), along_x(pair, -1)
    grads = [mine, ahead_g, along_x(ahead_g, 1), behind_g]
    grads += [pair, ahead_p, along_x(behind_p, -1), behind_p]

    attention, lse, far, *parts = call(
        forward_kernel,
        [
            shape(BLOCK, COLS),
            shape(HEADS_DEV, BLOCK, dtype=f32),
            shape(FAR_KEYS, 2 * COLS),
            *ring_shapes(2 * BLOCK, COLS),
        ],
        [
            vmem_q,
            vmem_w,
            pltpu.VMEM((FAR_KEYS + 2 * BLOCK, BLOCK), f32),
            smem_window,
            smem_window,
            smem_bias,
            dma((4,)),
        ],
        far=4,
        flops=4 * pair_flops * 3072,
        count=2 * BLOCK * 3072,
    )(near_window, mid_start, queries, out_weight, kv, prev_kv, *own_core, *other_core)
    keep, given = call(x_kernel, [shape(BLOCK, COLS, dtype=f32), shape(BLOCK, COLS)])(
        *ring(parts, along_x)
    )
    (layer_out,) = call(pair_kernel, [shape(BLOCK, COLS)])(keep, along_head(given, dz=1))

    grad_t = shape(COLS, BLOCK, dtype=f32)
    half_rows = FAR_KEYS // 2
    attention_grad, delta, dq, weight_own, sums_other = call(
        other_kernel,
        [
            shape(BLOCK, COLS),
            shape(HEADS_DEV, BLOCK, dtype=f32),
            grad_t,
            shape(half_rows, COLS),
            shape(half_rows, SUM_COLS),
        ],
        [vmem_q, vmem_w, smem_window, smem_bias, dma((3,))],
        far=3,
        flops=10 * pair_flops * 1024 + 4 * BLOCK * 2048 * COLS,
        count=2 * BLOCK * 1024,
    )(near_window, queries, out_weight, far, attention, lse, *grads)
    sums_got = along_seq(sums_other, dc=1)
    sums_own, dq = call(
        own_kernel,
        [shape(half_rows, SUM_COLS), grad_t],
        [vmem_q, smem_window, smem_bias, dma((2,))],
        far=2,
        flops=10 * pair_flops * 1024,
        count=2 * BLOCK * 1024,
    )(near_window, queries, far, lse, attention_grad, delta, dq, weight_own)
    parts = call(core_kernel, ring_shapes(CHUNK, SUM_COLS))(sums_own, sums_got)
    query_grad, near_grad, rim = call(
        near_kernel,
        [shape(BLOCK, COLS), shape(BLOCK, 2 * COLS, dtype=f32), shape(BLOCK, 2 * COLS)],
        [vmem_q, smem_window, dma((2,))],
        far=2,
        flops=10 * pair_flops * 1024,
        count=2 * BLOCK * 1024,
    )(near_window, queries, kv, prev_kv, lse, attention_grad, delta, dq)
    rim_got = passed_along(rim, -1)
    parts = call(y_kernel, ring_shapes(MIDS, SUM_COLS))(*ring(parts, along_y))
    key_grad, value_grad, weight_t = call(
        last_kernel,
        [shape(BLOCK, COLS), shape(BLOCK, COLS), shape(MIDS, COLS, dtype=f32)],
    )(*ring(parts, along_z), near_grad, rim_got)
    return layer_out, query_grad, key_grad, value_grad, weight_t.T


def solution(mesh):
    return jax.shard_map(
        on_device,
        mesh=mesh,
        in_specs=(
            P("seq", "head"),
            P("seq", "head"),
            P("seq", "head"),
            P("head", None),
            P("seq", "head"),
            P(),
            P(),
        ),
        out_specs=(
            P("seq", "head"),
            P("seq", "head"),
            P("seq", "head"),
            P("seq", "head"),
            P("head", "seq"),
        ),
        check_vma=False,
    )
```

```python
import math

import jax
import jax.numpy as jnp
from jax import lax
from jax.experimental import pallas as pl
from jax.experimental.pallas import tpu as pltpu
from jax.sharding import PartitionSpec as P

HEAD_DIM = 128
BLOCK = 512
POOL_MID = 8
MIDS = BLOCK // POOL_MID
HEADS_DEV = 2
COLS = HEADS_DEV * HEAD_DIM
Z, Y, C = 4, 4, 2
ZL, X = 2, 4
CHUNK = Z * MIDS
CHUNKS = Y * C
FAR_KEYS = CHUNKS * CHUNK
HALF = BLOCK // 2
SUM_COLS = 3 * COLS

NEGATIVE = -1e30
SCALING = HEAD_DIM ** (-0.5)
SCORE_SCALE = SCALING * math.log2(math.e)
MID_BIAS = math.log2(POOL_MID)

bf16 = jnp.bfloat16
f32 = jnp.float32


def along_seq(value, dz=0, dy=0, dc=0):
    pairs = []
    for z in range(Z):
        for y in range(Y):
            for c in range(C):
                target = (((z + dz) % Z) * Y + (y + dy) % Y) * C + (c + dc) % C
                pairs.append(((z * Y + y) * C + c, target))
    return lax.ppermute(value, "seq", pairs)


def along_head(value, dz=0, dx=0):
    pairs = []
    for z in range(ZL):
        for x in range(X):
            pairs.append((z * X + x, ((z + dz) % ZL) * X + (x + dx) % X))
    return lax.ppermute(value, "head", pairs)


def along_z(value, step):
    return along_seq(value, dz=step)


def along_y(value, step):
    return along_seq(value, dy=step)


def along_x(value, step):
    return along_head(value, dx=step)


def passed_along(value, steps):
    count = Z * Y * C
    initial, last = (max(0, -steps), min(count, count - steps))
    return lax.ppermute(value, "seq", [(source, source + steps) for source in range(initial, last)])


def shape(*dims, dtype=bf16):
    return jax.ShapeDtypeStruct(dims, dtype)


def call(kernel, outs, scratch=(), far=0, flops=0, count=0, after=()):
    def run(*args):
        moved = sum(a.size * a.dtype.itemsize for a in (*args, *outs))

        def body(*refs):
            kernel(*refs[: len(args)], *refs[len(args) + len(after) :])

        return pl.pallas_call(
            body,
            out_shape=list(outs),
            in_specs=[pl.BlockSpec(memory_space=pl.ANY)] * far
            + [pl.BlockSpec(memory_space=pltpu.VMEM)] * (len(args) - far)
            + [pl.BlockSpec(memory_space=pl.ANY)] * len(after),
            out_specs=[pl.BlockSpec(memory_space=pltpu.VMEM)] * len(outs),
            scratch_shapes=list(scratch),
            cost_estimate=pl.CostEstimate(flops=flops, bytes_accessed=moved, transcendentals=count),
            compiler_params=pltpu.CompilerParams(vmem_limit_bytes=26 * 1024 * 1024),
        )(*args, *after)

    return run


def place():
    s = lax.axis_index("seq")
    return s, s >> 3, (s >> 1) & 3, s & 1


def block_of(z, y, c, group, dz):
    core = (c + (group >> 2)) & 1
    return ((z - dz) & 3) * 8 + ((y - group) & 3) * 2 + core


def dot(a, b, da, db):
    return lax.dot_general(a, b, (((da,), (db,)), ((), ())), preferred_element_type=f32)


def wide(ref, rows):
    return ref[rows].astype(f32)


def emit(chunk, outs):
    behind, ahead, late_behind, late_ahead, own = outs
    h = chunk(0).shape[0] // 2
    behind[:h], behind[h:] = chunk(1)[h:], chunk(2)[:h]
    ahead[:h], ahead[h:] = chunk(3)[:h], chunk(2)[h:]
    late_behind[...], late_ahead[...] = chunk(1)[:h], chunk(3)[h:]
    own[...] = chunk(0)


def ring_shapes(rows, width):
    h = rows // 2
    return [shape(rows, width)] * 2 + [shape(h, width)] * 2 + [shape(rows, width)]


def turn_kernel(late_behind, late_ahead, got_behind, got_ahead, out_behind, out_ahead):
    h = late_behind.shape[0]
    rest, all_rows = slice(h, 2 * h), slice(0, h)
    out_behind[...] = (wide(late_behind, all_rows) + wide(got_behind, rest)).astype(bf16)
    out_ahead[...] = (wide(late_ahead, all_rows) + wide(got_ahead, rest)).astype(bf16)


def ring(parts, along, after=()):
    behind, ahead, late_behind, late_ahead, own = parts
    got_behind, got_ahead = along(behind, -1), along(ahead, 1)
    turned = [shape(*late_behind.shape)] * 2
    out_behind, out_ahead = call(turn_kernel, turned, after=after)(
        late_behind, late_ahead, got_behind, got_ahead
    )
    return own, got_behind, got_ahead, along(out_behind, -1), along(out_ahead, 1)


def halves(own, got_behind, got_ahead, last_behind, last_ahead):
    h = last_behind.shape[0]
    first, rest = slice(0, h), slice(h, 2 * h)
    a = wide(own, first) + wide(got_ahead, first) + wide(last_behind, first)
    b = wide(own, rest) + wide(got_behind, first) + wide(last_ahead, first)
    return a, b


def pool_kernel(k_hbm, v_hbm, kv_ref, mid_ref, sems):
    copies = [
        pltpu.make_async_copy(k_hbm, kv_ref.at[:, :COLS], sems.at[0]),
        pltpu.make_async_copy(v_hbm, kv_ref.at[:, COLS:], sems.at[1]),
    ]
    for copy in copies:
        copy.start()
    row = lax.broadcasted_iota(jnp.int32, (MIDS, BLOCK), 0)
    col = lax.broadcasted_iota(jnp.int32, (MIDS, BLOCK), 1)
    mean = jnp.where(row == col // POOL_MID, 1.0 / POOL_MID, 0.0).astype(bf16)
    for copy in copies:
        copy.wait()
    mid_ref[...] = dot(mean, kv_ref[...], 1, 0).astype(bf16)


def gather_kernel(mid_ref, a, b, c, kv_ref, run_ref, kv_out):
    for i, ref in enumerate((mid_ref, a, b, c)):
        run_ref[i * MIDS : (i + 1) * MIDS] = ref[...]
    kv_out[...] = kv_ref[...]


def part_kernel(run_ref, ahead_ref, behind_ref, three_ref, first_ref, rest_ref):
    h = CHUNK // 2
    for i, ref in enumerate((run_ref, ahead_ref, behind_ref)):
        three_ref[i * CHUNK : (i + 1) * CHUNK] = ref[...]
    first_ref[...] = ahead_ref[:h]
    rest_ref[...] = behind_ref[h:]


def own_mask(first_key):
    key = lax.broadcasted_iota(jnp.int32, (HALF, BLOCK), 0) + first_key
    query = lax.broadcasted_iota(jnp.int32, (HALF, BLOCK), 1)
    return key <= query


def chunk_bias(bias_ref, g, scores):
    return jnp.concatenate(
        [scores[d * MIDS : (d + 1) * MIDS] + bias_ref[g * Z + d] for d in range(Z)], axis=0
    )


def chunk_rows(g):
    return pl.ds(pl.multiple_of(g * CHUNK, CHUNK), CHUNK)


def head_cols(h):
    return slice(h * HEAD_DIM, (h + 1) * HEAD_DIM), slice(
        COLS + h * HEAD_DIM, COLS + (h + 1) * HEAD_DIM
    )


def weight_cols(zl, x, dx, dz):
    device = ((zl + dz) & 1) * X + ((x - dx) & 3)
    return device, pl.ds(pl.multiple_of(device * COLS, COLS), COLS)


def forward_kernel(
    nw_hbm, ms_hbm, q_ref, w_ref, kv_ref, pkv_ref, *refs
):
    mids = []
    for three, first, rest in (refs[:3], refs[3:6]):
        runs = [three[i * CHUNK : (i + 1) * CHUNK] for i in range(3)]
        mids += [runs[0], runs[1], jnp.concatenate([first[...], rest[...]], axis=0), runs[2]]
    att_ref, lse_ref, far_ref, *outs = refs[6:14]
    s_ref, nw_ref, ms_ref, bias_ref, sems = refs[14:]
    copies = [
        pltpu.make_async_copy(a, b, sems.at[i])
        for i, (a, b) in enumerate(((nw_hbm, nw_ref), (ms_hbm, ms_ref)))
    ]
    for copy in copies:
        copy.start()
    s, z, y, c = place()
    row = lax.broadcasted_iota(jnp.int32, (CHUNK, CHUNK), 0)
    col = lax.broadcasted_iota(jnp.int32, (CHUNK, CHUNK), 1)
    same = jnp.where(row == col, 1.0, 0.0)
    mean = jnp.where(row // POOL_MID == col // POOL_MID, 1.0 / POOL_MID, 0.0)
    for copy in copies:
        copy.wait()
    near_begin = jnp.maximum(s + 1 - nw_ref[s], 0)
    mid_begin = jnp.minimum(ms_ref[s], near_begin)
    for g in range(CHUNKS):
        picks = []
        for dz in range(Z):
            b = block_of(z, y, c, g, dz)
            bias_ref[g * Z + dz] = jnp.where(b < near_begin, MID_BIAS, NEGATIVE)
            far = jnp.where(b < mid_begin, 1.0, 0.0)
            rows = slice(dz * MIDS, (dz + 1) * MIDS)
            picks.append(same[rows] + far * (mean[rows] - same[rows]))
        pick = jnp.concatenate(picks, axis=0).astype(bf16)
        far_ref[g * CHUNK : (g + 1) * CHUNK, :] = dot(pick, mids[g], 1, 0).astype(bf16)
    prev_bias = jnp.where(near_begin < s, 0.0, NEGATIVE)
    for h in range(HEADS_DEV):
        cols, vcols = head_cols(h)
        q = q_ref[:, cols]
        top = jnp.full((1, BLOCK), NEGATIVE, f32)
        for part in range(4):
            keys = (kv_ref, pkv_ref)[part // 2][(part % 2) * HALF : (part % 2 + 1) * HALF, cols]
            sc = dot(keys, q, 1, 1) * SCORE_SCALE
            if part < 2:
                sc = jnp.where(own_mask(part * HALF), sc, NEGATIVE)
            else:
                sc = sc + prev_bias
            s_ref[FAR_KEYS + part * HALF : FAR_KEYS + (part + 1) * HALF, :] = sc
            top = jnp.maximum(top, jnp.max(sc, axis=0, keepdims=True))

        def scores(g, top):
            rows = chunk_rows(g)
            sc = chunk_bias(bias_ref, g, dot(far_ref[rows, cols], q, 1, 1) * SCORE_SCALE)
            s_ref[rows, :] = sc
            return jnp.maximum(top, jnp.max(sc, axis=0, keepdims=True))

        top = lax.fori_loop(0, CHUNKS, scores, top, unroll=2)

        def step(score, values):
            e = jnp.exp2(score - top)
            return jnp.sum(e, axis=0, keepdims=True), dot(values, e.astype(bf16), 0, 0)

        def gather(g, carry):
            a, b = step(s_ref[chunk_rows(g), :], far_ref[chunk_rows(g), vcols])
            return carry[0] + a, carry[1] + b

        start = (jnp.zeros((1, BLOCK), f32), jnp.zeros((HEAD_DIM, BLOCK), f32))
        sums, out = lax.fori_loop(0, CHUNKS, gather, start, unroll=2)
        for part in range(4):
            values = (kv_ref, pkv_ref)[part // 2][(part % 2) * HALF : (part % 2 + 1) * HALF, vcols]
            rows = slice(FAR_KEYS + part * HALF, FAR_KEYS + (part + 1) * HALF)
            a, b = step(s_ref[rows, :], values)
            sums, out = sums + a, out + b
        att_ref[:, cols] = (out / sums).T.astype(bf16)
        lse_ref[h : h + 1, :] = top + jnp.log2(sums)
    me = lax.axis_index("head")
    zl, x = me >> 2, me & 3

    def projected(dx, dz):
        columns = weight_cols(zl, x, dx, dz)[1]
        return dot(att_ref[...], w_ref[:, columns], 1, 0).astype(bf16)

    behind, ahead, late_behind, late_ahead, own = outs
    behind[:BLOCK], behind[BLOCK:] = projected(1, 1), projected(2, 0)
    ahead[:BLOCK], ahead[BLOCK:] = projected(3, 0), projected(2, 1)
    late_behind[...], late_ahead[...] = projected(1, 0), projected(3, 1)
    own[:BLOCK], own[BLOCK:] = projected(0, 0), projected(0, 1)


def step(keys, values, q, do, lse, delta, bias):
    w = jnp.exp2(bias(dot(keys, q, 1, 1) * SCORE_SCALE) - lse)
    ds = (w * (dot(values, do, 1, 1) - delta)).astype(bf16)
    dv = dot(w.astype(bf16), do, 1, 0)
    dk = dot(ds, q, 1, 0) * SCALING
    return dk, dv, dot(keys, ds, 0, 0)


def far_part(first, refs, bias_ref, near_begin, out_ref, dq_in, dq_out):
    q_ref, far_ref, lse_ref, do_ref, delta_ref = refs
    s, z, y, c = place()
    for g in range(first, first + Y):
        for dz in range(Z):
            b = block_of(z, y, c, g, dz)
            bias_ref[g * Z + dz] = jnp.where(b < near_begin, MID_BIAS, NEGATIVE)
    for h in range(HEADS_DEV):
        cols, vcols = head_cols(h)
        q, do = q_ref[:, cols], do_ref[:, cols]
        lse, delta = lse_ref[h : h + 1, :], delta_ref[h : h + 1, :]

        def body(i, acc):
            g = i + first
            rows = chunk_rows(g)
            dk, dv, dq = step(
                far_ref[rows, cols], far_ref[rows, vcols], q, do, lse, delta,
                lambda sc: chunk_bias(bias_ref, g, sc),
            )
            out_ref[chunk_rows(i), cols] = dk.astype(bf16)
            out_ref[chunk_rows(i), vcols] = dv.astype(bf16)
            return acc + dq

        acc = jnp.zeros((HEAD_DIM, BLOCK), f32) if dq_in is None else dq_in[cols, :]
        dq_out[cols, :] = lax.fori_loop(0, Y, body, acc, unroll=2)


def other_kernel(nw_hbm, q_ref, w_ref, far_ref, att_ref, lse_ref, *refs):
    grads = refs[: ZL * X]
    do_ref, delta_ref, dq_ref, weight_ref, out_ref, nw_ref, bias_ref, sems = refs[ZL * X :]
    copy = pltpu.make_async_copy(nw_hbm, nw_ref, sems.at[0])
    copy.start()
    s, z, y, c = place()
    me = lax.axis_index("head")
    zl, x = me >> 2, me & 3
    acc = jnp.zeros((BLOCK, COLS), f32)
    for i in range(ZL * X):
        device, columns = weight_cols(zl, x, i % X, i // X)
        grad = grads[i][...]
        acc = acc + dot(grad, w_ref[:, columns], 1, 1)
        term = dot(grad, att_ref[...], 0, 0).astype(bf16)
        for part in range(COLS // MIDS):
            block = device * (COLS // MIDS) + part
            bz, by = block >> 3, (block >> 1) & 3
            row = pl.multiple_of((((y - by) & 3) * Z + ((z - bz) & 3)) * MIDS, MIDS)
            piece = term[part * MIDS : (part + 1) * MIDS]

            @pl.when(c == part % 2)
            def _():
                weight_ref[pl.ds(row, MIDS), :] = piece

            @pl.when(c != part % 2)
            def _():
                out_ref[pl.ds(row, MIDS), 2 * COLS :] = piece

    do_ref[...] = acc.astype(bf16)
    for h in range(HEADS_DEV):
        cols, _ = head_cols(h)
        product = do_ref[:, cols].astype(f32) * att_ref[:, cols].astype(f32)
        delta_ref[h : h + 1, :] = jnp.sum(product.T, axis=0, keepdims=True)
    copy.wait()
    near_begin = jnp.maximum(s + 1 - nw_ref[s], 0)
    parts = (q_ref, far_ref, lse_ref, do_ref, delta_ref)
    far_part(Y, parts, bias_ref, near_begin, out_ref, None, dq_ref)


def own_kernel(
    nw_hbm, q_ref, far_ref, lse_ref, do_ref, delta_ref, dq_in, weight_ref, out_ref, dq_ref,
    nw_ref, bias_ref, sems,
):
    copy = pltpu.make_async_copy(nw_hbm, nw_ref, sems.at[0])
    copy.start()
    out_ref[:, 2 * COLS :] = weight_ref[...]
    copy.wait()
    s = place()[0]
    near_begin = jnp.maximum(s + 1 - nw_ref[s], 0)
    parts = (q_ref, far_ref, lse_ref, do_ref, delta_ref)
    far_part(0, parts, bias_ref, near_begin, out_ref, dq_in, dq_ref)


def prev_kernel(
    nw_hbm, q_ref, pkv_ref, lse_ref, do_ref, delta_ref, dq_in, rim_ref, dq_ref, nw_ref, sems
):
    copy = pltpu.make_async_copy(nw_hbm, nw_ref, sems.at[0])
    copy.start()
    copy.wait()
    s = place()[0]
    near_begin = jnp.maximum(s + 1 - nw_ref[s], 0)
    prev_bias = jnp.where(near_begin < s, 0.0, NEGATIVE)
    for h in range(HEADS_DEV):
        cols, vcols = head_cols(h)
        q, do = q_ref[:, cols], do_ref[:, cols]
        lse, delta = lse_ref[h : h + 1, :], delta_ref[h : h + 1, :]
        acc = dq_in[cols, :]
        for part in range(2):
            rows = slice(part * HALF, (part + 1) * HALF)
            dk, dv, dq = step(
                pkv_ref[rows, cols], pkv_ref[rows, vcols], q, do, lse, delta,
                lambda sc: sc + prev_bias,
            )
            rim_ref[rows, cols] = dk.astype(bf16)
            rim_ref[rows, vcols] = dv.astype(bf16)
            acc = acc + dq
        dq_ref[cols, :] = acc


def near_kernel(q_ref, kv_ref, lse_ref, do_ref, delta_ref, dq_in, dq_ref, near_ref):
    for h in range(HEADS_DEV):
        cols, vcols = head_cols(h)
        q, do = q_ref[:, cols], do_ref[:, cols]
        lse, delta = lse_ref[h : h + 1, :], delta_ref[h : h + 1, :]
        acc = dq_in[cols, :]
        for part in range(2):
            rows = slice(part * HALF, (part + 1) * HALF)
            dk, dv, dq = step(
                kv_ref[rows, cols], kv_ref[rows, vcols], q, do, lse, delta,
                lambda sc: jnp.where(own_mask(part * HALF), sc, NEGATIVE),
            )
            near_ref[rows, cols] = dk
            near_ref[rows, vcols] = dv
            acc = acc + dq
        dq_ref[:, cols] = (acc * SCALING).T.astype(bf16)


def core_kernel(own_ref, got_ref, *outs):
    def chunk(i):
        rows = slice(i * CHUNK, (i + 1) * CHUNK)
        return (wide(own_ref, rows) + wide(got_ref, rows)).astype(bf16)

    emit(chunk, outs)


def y_kernel(*refs):
    a, b = halves(*refs[:5])
    both = [h[i * MIDS : (i + 1) * MIDS].astype(bf16) for h in (a, b) for i in range(2)]
    emit(lambda i: both[i], refs[5:])


def x_kernel(own, got_behind, got_ahead, last_behind, last_ahead, keep_ref, pass_ref):
    a, b = halves(own, got_behind, got_ahead, last_behind, last_ahead)
    keep_ref[...] = a
    pass_ref[...] = b.astype(bf16)


def pair_kernel(keep_ref, got_ref, out_ref):
    out_ref[...] = (keep_ref[...] + got_ref[...].astype(f32)).astype(bf16)


def last_kernel(own, got_behind, got_ahead, last_behind, last_ahead, near_ref, rim_ref, key_ref, value_ref, weight_ref):
    total = jnp.concatenate(
        halves(own, got_behind, got_ahead, last_behind, last_ahead), axis=0
    )
    weight_ref[...] = total[:, 2 * COLS :]
    mid = total[:, : 2 * COLS] * (1.0 / POOL_MID)
    spread = jnp.broadcast_to(mid[:, None, :], (MIDS, POOL_MID, 2 * COLS)).reshape(BLOCK, 2 * COLS)
    grad = near_ref[...] + rim_ref[...].astype(f32) + spread
    key_ref[...] = grad[:, :COLS].astype(bf16)
    value_ref[...] = grad[:, COLS:].astype(bf16)


def on_device(queries, key_frames, value_frames, out_weight, out_grad, near_window, mid_start):
    dma = pltpu.SemaphoreType.DMA
    smem_window = pltpu.SMEM((Z * Y * C,), jnp.int32)
    smem_bias = pltpu.SMEM((CHUNKS * Z,), f32)
    pair_flops = 2 * HEADS_DEV * BLOCK * HEAD_DIM

    kv, mid = call(
        pool_kernel, [shape(BLOCK, 2 * COLS), shape(MIDS, 2 * COLS)], [dma((2,))], far=2
    )(key_frames, value_frames)
    ahead_g, behind_g = along_x(out_grad, 1), along_x(out_grad, -1)
    run, kv_sent = call(
        gather_kernel,
        [shape(CHUNK, 2 * COLS), shape(BLOCK, 2 * COLS)],
        after=(ahead_g, behind_g),
    )(mid, *[along_z(mid, i) for i in range(1, Z)], kv)
    ahead, behind = along_y(run, 1), along_y(run, -1)
    prev_kv = passed_along(kv_sent, 1)
    beyond_g = along_x(ahead_g, 1)
    pair = along_head(out_grad, dz=1)
    three, first, rest = call(
        part_kernel,
        [shape(3 * CHUNK, 2 * COLS), *[shape(CHUNK // 2, 2 * COLS)] * 2],
        after=(beyond_g, pair),
    )(run, ahead, behind)
    own_core = [three, along_y(first, 1), along_y(rest, -1)]
    other_core = [along_seq(v, dc=1) for v in own_core]
    ahead_p, behind_p = along_x(pair, 1), along_x(pair, -1)
    beyond_p = along_x(behind_p, -1)
    grads = [out_grad, ahead_g, beyond_g, behind_g, pair, ahead_p, beyond_p, behind_p]

    attention, lse, far, *parts = call(
        forward_kernel,
        [
            shape(BLOCK, COLS),
            shape(HEADS_DEV, BLOCK, dtype=f32),
            shape(FAR_KEYS, 2 * COLS),
            *ring_shapes(2 * BLOCK, COLS),
        ],
        [
            pltpu.VMEM((FAR_KEYS + 2 * BLOCK, BLOCK), f32),
            smem_window,
            smem_window,
            smem_bias,
            dma((2,)),
        ],
        far=2,
        flops=4 * pair_flops * 3072,
        count=2 * BLOCK * 3072,
        after=(ahead_p, behind_p),
    )(near_window, mid_start, queries, out_weight, kv, prev_kv, *own_core, *other_core)

    grad_t = shape(COLS, BLOCK, dtype=f32)
    half_rows = FAR_KEYS // 2
    attention_grad, delta, dq, weight_own, sums_other = call(
        other_kernel,
        [
            shape(BLOCK, COLS),
            shape(HEADS_DEV, BLOCK, dtype=f32),
            grad_t,
            shape(half_rows, COLS),
            shape(half_rows, SUM_COLS),
        ],
        [smem_window, smem_bias, dma((1,))],
        far=1,
        flops=10 * pair_flops * 1024 + 4 * BLOCK * 2048 * COLS,
        count=2 * BLOCK * 1024,
    )(near_window, queries, out_weight, far, attention, lse, *grads)
    sums_got = along_seq(sums_other, dc=1)
    rim, dq = call(
        prev_kernel,
        [shape(BLOCK, 2 * COLS), grad_t],
        [smem_window, dma((1,))],
        far=1,
        flops=10 * pair_flops * 512,
        count=2 * BLOCK * 512,
    )(near_window, queries, prev_kv, lse, attention_grad, delta, dq)
    rim_got = passed_along(rim, -1)
    sums_own, dq = call(
        own_kernel,
        [shape(half_rows, SUM_COLS), grad_t],
        [smem_window, smem_bias, dma((1,))],
        far=1,
        flops=10 * pair_flops * 1024,
        count=2 * BLOCK * 1024,
    )(near_window, queries, far, lse, attention_grad, delta, dq, weight_own)
    sums = call(core_kernel, ring_shapes(CHUNK, SUM_COLS))(sums_own, sums_got)
    query_grad, near_grad = call(
        near_kernel,
        [shape(BLOCK, COLS), shape(BLOCK, 2 * COLS, dtype=f32)],
        flops=10 * pair_flops * 512,
        count=2 * BLOCK * 512,
        after=(sums[0],),
    )(queries, kv, lse, attention_grad, delta, dq)

    parts = ring(parts, along_x, after=(near_grad,))
    sums = ring(sums, along_y, after=(near_grad,))
    keep, given = call(x_kernel, [shape(BLOCK, COLS, dtype=f32), shape(BLOCK, COLS)])(*parts)
    given = along_head(given, dz=1)
    sums = call(y_kernel, ring_shapes(MIDS, SUM_COLS))(*sums)
    sums = ring(sums, along_z)
    (layer_out,) = call(pair_kernel, [shape(BLOCK, COLS)])(keep, given)
    key_grad, value_grad, weight_t = call(
        last_kernel,
        [shape(BLOCK, COLS), shape(BLOCK, COLS), shape(MIDS, COLS, dtype=f32)],
    )(*sums, near_grad, rim_got)
    return layer_out, query_grad, key_grad, value_grad, weight_t.T


def solution(mesh):
    return jax.shard_map(
        on_device,
        mesh=mesh,
        in_specs=(
            P("seq", "head"),
            P("seq", "head"),
            P("seq", "head"),
            P("head", None),
            P("seq", "head"),
            P(),
            P(),
        ),
        out_specs=(
            P("seq", "head"),
            P("seq", "head"),
            P("seq", "head"),
            P("seq", "head"),
            P("head", "seq"),
        ),
        check_vma=False,
    )
```

```python
import functools
import math

import jax
import jax.numpy as jnp
from jax import lax
from jax.experimental import pallas as pl
from jax.experimental.pallas import tpu as pltpu
from jax.sharding import PartitionSpec as P

HEAD_DIM = 128
BLOCK = 512
POOL_MID = 8
MIDS = BLOCK // POOL_MID
HEADS_DEV = 2
COLS = HEADS_DEV * HEAD_DIM
Z, Y, C = 4, 4, 2
ZL, X = 2, 4
CHUNK = Z * MIDS
CHUNKS = Y * C
FAR_KEYS = CHUNKS * CHUNK
HALF = BLOCK // 2
SUM_COLS = 3 * COLS

NEGATIVE = -1e30
SCALING = HEAD_DIM ** (-0.5)
SCORE_SCALE = SCALING * math.log2(math.e)
MID_BIAS = math.log2(POOL_MID)

bf16 = jnp.bfloat16
f32 = jnp.float32


def along_seq(value, dz=0, dy=0, dc=0):
    pairs = []
    for z in range(Z):
        for y in range(Y):
            for c in range(C):
                target = (((z + dz) % Z) * Y + (y + dy) % Y) * C + (c + dc) % C
                pairs.append(((z * Y + y) * C + c, target))
    return lax.ppermute(value, "seq", pairs)


def along_head(value, dz=0, dx=0):
    pairs = []
    for z in range(ZL):
        for x in range(X):
            pairs.append((z * X + x, ((z + dz) % ZL) * X + (x + dx) % X))
    return lax.ppermute(value, "head", pairs)


def along_z(value, step):
    return along_seq(value, dz=step)


def along_y(value, step):
    return along_seq(value, dy=step)


def along_x(value, step):
    return along_head(value, dx=step)


def passed_along(value, steps):
    count = Z * Y * C
    initial, last = (max(0, -steps), min(count, count - steps))
    return lax.ppermute(value, "seq", [(source, source + steps) for source in range(initial, last)])


def shape(*dims, dtype=bf16):
    return jax.ShapeDtypeStruct(dims, dtype)


def call(kernel, outs, scratch=(), far=0, flops=0, count=0, after=()):
    def run(*args):
        moved = sum(a.size * a.dtype.itemsize for a in (*args, *outs))

        def body(*refs):
            kernel(*refs[: len(args)], *refs[len(args) + len(after) :])

        return pl.pallas_call(
            body,
            out_shape=list(outs),
            in_specs=[pl.BlockSpec(memory_space=pltpu.HBM)] * far
            + [pl.BlockSpec(memory_space=pltpu.VMEM)] * (len(args) - far)
            + [pl.BlockSpec(memory_space=pl.ANY)] * len(after),
            out_specs=[pl.BlockSpec(memory_space=pltpu.VMEM)] * len(outs),
            scratch_shapes=list(scratch),
            cost_estimate=pl.CostEstimate(flops=flops, bytes_accessed=moved, transcendentals=count),
            compiler_params=pltpu.CompilerParams(vmem_limit_bytes=26 * 1024 * 1024),
        )(*args, *after)

    return run


def place():
    s = lax.axis_index("seq")
    return s, s >> 3, (s >> 1) & 3, s & 1


def block_of(z, y, c, group, dz):
    core = (c + (group >> 2)) & 1
    return ((z - dz) & 3) * 8 + ((y - group) & 3) * 2 + core


def behind_y(i):
    return i ^ (i >> 1)


def dot(a, b, da, db):
    return lax.dot_general(a, b, (((da,), (db,)), ((), ())), preferred_element_type=f32)


def wide(ref, rows):
    return ref[rows].astype(f32)


def emit(chunk, outs):
    behind, ahead, late_behind, late_ahead, own = outs
    h = chunk(0).shape[0] // 2
    behind[:h], behind[h:] = chunk(1)[h:], chunk(2)[:h]
    ahead[:h], ahead[h:] = chunk(3)[:h], chunk(2)[h:]
    late_behind[...], late_ahead[...] = chunk(1)[:h], chunk(3)[h:]
    own[...] = chunk(0)


def ring_shapes(rows, width):
    h = rows // 2
    return [shape(rows, width)] * 2 + [shape(h, width)] * 2 + [shape(rows, width)]


def turn_kernel(late_behind, late_ahead, got_behind, got_ahead, out_behind, out_ahead):
    h = late_behind.shape[0]
    rest, all_rows = slice(h, 2 * h), slice(0, h)
    out_behind[...] = (wide(late_behind, all_rows) + wide(got_behind, rest)).astype(bf16)
    out_ahead[...] = (wide(late_ahead, all_rows) + wide(got_ahead, rest)).astype(bf16)


def ring(parts, along, after=()):
    behind, ahead, late_behind, late_ahead, own = parts
    got_behind, got_ahead = along(behind, -1), along(ahead, 1)
    turned = [shape(*late_behind.shape)] * 2
    out_behind, out_ahead = call(turn_kernel, turned, after=after)(
        late_behind, late_ahead, got_behind, got_ahead
    )
    sent = along(out_behind, -1), along(out_ahead, 1)
    return (own, got_behind, got_ahead, *sent), out_behind


def halves(own, got_behind, got_ahead, last_behind, last_ahead):
    h = last_behind.shape[0]
    first, rest = slice(0, h), slice(h, 2 * h)
    a = wide(own, first) + wide(got_ahead, first) + wide(last_behind, first)
    b = wide(own, rest) + wide(got_behind, first) + wide(last_ahead, first)
    return a, b


def pool_kernel(kv_ref, mid_ref):
    row = lax.broadcasted_iota(jnp.int32, (MIDS, BLOCK), 0)
    col = lax.broadcasted_iota(jnp.int32, (MIDS, BLOCK), 1)
    mean = jnp.where(row == col // POOL_MID, 1.0 / POOL_MID, 0.0).astype(bf16)
    mid_ref[...] = dot(mean, kv_ref[...], 1, 0).astype(bf16)


def gather_kernel(mid_ref, a, b, c, grad_ref, pair_ref, run_ref, grads_out):
    for i, ref in enumerate((mid_ref, a, b, c)):
        run_ref[i * MIDS : (i + 1) * MIDS] = ref[...]
    grads_out[:BLOCK] = grad_ref[...]
    grads_out[BLOCK:] = pair_ref[...]


def part_kernel(run_ref, ahead_ref, behind_ref, kv_ref, first_ref, rest_ref, three_ref, keys_out):
    h = CHUNK // 2
    first_ref[...] = ahead_ref[:h]
    rest_ref[...] = behind_ref[h:]
    for i, ref in enumerate((run_ref, ahead_ref, behind_ref)):
        three_ref[i * CHUNK : (i + 1) * CHUNK] = ref[...]
    keys_out[...] = kv_ref[:, :COLS]


def join_kernel(first, rest, grads_1, grads_3, last_ref, own_out, pair_out):
    last_ref[: CHUNK // 2] = first[...]
    last_ref[CHUNK // 2 :] = rest[...]
    own_out[...] = grads_1[:BLOCK]
    pair_out[...] = grads_3[BLOCK:]


def own_mask(first_key):
    key = lax.broadcasted_iota(jnp.int32, (HALF, BLOCK), 0) + first_key
    query = lax.broadcasted_iota(jnp.int32, (HALF, BLOCK), 1)
    return key <= query


def chunk_exponents(bias_ref, g, product, top):
    return jnp.concatenate(
        [
            product[d * MIDS : (d + 1) * MIDS] * SCORE_SCALE + (bias_ref[g * Z + d] - top)
            for d in range(Z)
        ],
        axis=0,
    )


def chunk_rows(g):
    return pl.ds(pl.multiple_of(g * CHUNK, CHUNK), CHUNK)


def head_cols(h):
    return slice(h * HEAD_DIM, (h + 1) * HEAD_DIM), slice(
        COLS + h * HEAD_DIM, COLS + (h + 1) * HEAD_DIM
    )


def weight_cols(zl, x, dx, dz):
    device = ((zl + dz) & 1) * X + ((x - dx) & 3)
    return device, pl.ds(pl.multiple_of(device * COLS, COLS), COLS)


def effective(near_begin, mid_begin, chunks, bias_ref):
    s, z, y, c = place()
    row = lax.broadcasted_iota(jnp.int32, (CHUNK, CHUNK), 0)
    col = lax.broadcasted_iota(jnp.int32, (CHUNK, CHUNK), 1)
    same = jnp.where(row == col, 1.0, 0.0)
    mean = jnp.where(row // POOL_MID == col // POOL_MID, 1.0 / POOL_MID, 0.0)
    for i, (core, number, mids_ref, mids_row, far_ref, far_row) in enumerate(chunks):
        picks = []
        for dz in range(Z):
            b = block_of(z, y, c, core * Y + behind_y(number), dz)
            bias_ref[i * Z + dz] = jnp.where(b < near_begin, MID_BIAS, NEGATIVE)
            far = jnp.where(b < mid_begin, 1.0, 0.0)
            rows = slice(dz * MIDS, (dz + 1) * MIDS)
            picks.append(same[rows] + far * (mean[rows] - same[rows]))
        pick = jnp.concatenate(picks, axis=0).astype(bf16)
        mids = mids_ref[mids_row : mids_row + CHUNK, :]
        far_ref[far_row : far_row + CHUNK, :] = dot(pick, mids, 1, 0).astype(bf16)


def window(nw_hbm, ms_hbm, nw_ref, ms_ref, sems):
    copies = [
        pltpu.make_async_copy(a, b, sems.at[i])
        for i, (a, b) in enumerate(((nw_hbm, nw_ref), (ms_hbm, ms_ref)))
    ]
    for copy in copies:
        copy.start()
    for copy in copies:
        copy.wait()
    s = place()[0]
    near_begin = jnp.maximum(s + 1 - nw_ref[s], 0)
    return near_begin, jnp.minimum(ms_ref[s], near_begin)


def level(h, q_t, near_ref, near_mask, near_bias, chunks, bias_ref, s_ref):
    cols, vcols = head_cols(h)
    top = jnp.full((1, BLOCK), 0.1 * NEGATIVE, f32)

    def highest(top, product, bias):
        return jnp.maximum(top, jnp.max(product, axis=0, keepdims=True) * SCORE_SCALE + bias)

    for part in range(2):
        rows = slice(part * HALF, (part + 1) * HALF)
        product = dot(near_ref[rows, cols], q_t, 1, 0)
        if near_mask:
            product = jnp.where(own_mask(part * HALF), product, NEGATIVE)
        s_ref[rows, :] = product
        top = highest(top, product, near_bias)

    for g, (_, _, _, _, far_ref, row) in enumerate(chunks):
        product = dot(far_ref[row : row + CHUNK, cols], q_t, 1, 0)
        s_ref[BLOCK + g * CHUNK : BLOCK + (g + 1) * CHUNK, :] = product
        for d in range(Z):
            top = highest(top, product[d * MIDS : (d + 1) * MIDS], bias_ref[g * Z + d])

    def values_of(exponents, values):
        e = jnp.exp2(exponents)
        return jnp.sum(e, axis=0, keepdims=True), dot(values, e.astype(bf16), 0, 0)

    sums, out = jnp.zeros((1, BLOCK), f32), jnp.zeros((HEAD_DIM, BLOCK), f32)
    for g, (_, _, _, _, far_ref, row) in enumerate(chunks):
        product = s_ref[BLOCK + g * CHUNK : BLOCK + (g + 1) * CHUNK, :]
        exponents = chunk_exponents(bias_ref, g, product, top)
        a, b = values_of(exponents, far_ref[row : row + CHUNK, vcols])
        sums, out = sums + a, out + b
    for part in range(2):
        rows = slice(part * HALF, (part + 1) * HALF)
        a, b = values_of(s_ref[rows, :] * SCORE_SCALE + (near_bias - top), near_ref[rows, vcols])
        sums, out = sums + a, out + b
    return top, sums, out


def first_kernel(
    nw_hbm, ms_hbm, q_ref, kv_ref, mids_ref, far_ref, top_ref, sums_ref, out_ref,
    s_ref, nw_ref, ms_ref, bias_ref, sems,
):
    near_begin, mid_begin = window(nw_hbm, ms_hbm, nw_ref, ms_ref, sems)
    chunks = [(0, i, mids_ref, i * CHUNK, far_ref, i * CHUNK) for i in range(3)]
    effective(near_begin, mid_begin, chunks, bias_ref)
    for h in range(HEADS_DEV):
        top, sums, out = level(
            h, q_ref[:, head_cols(h)[0]].T, kv_ref, True, 0.0, chunks, bias_ref, s_ref
        )
        top_ref[h : h + 1, :] = top
        sums_ref[h : h + 1, :] = sums
        out_ref[head_cols(h)[0], :] = out


def second_kernel(
    nw_hbm, ms_hbm, q_ref, w_ref, pk_ref, pv_ref, last_ref, three_ref, other_ref, far_own_ref,
    top_ref, sums_ref, out_ref, far_last_ref, far_ref, pkv_ref, att_ref, lse_ref, behind, ahead, late_behind, late_ahead, own,
    s_ref, nw_ref, ms_ref, bias_ref, sems,
):
    near_begin, mid_begin = window(nw_hbm, ms_hbm, nw_ref, ms_ref, sems)
    chunks = [(0, 3, last_ref, 0, far_last_ref, 3 * CHUNK)]
    chunks += [(1, i, three_ref, i * CHUNK, far_ref, i * CHUNK) for i in range(3)]
    chunks += [(1, 3, other_ref, 0, far_ref, 3 * CHUNK)]
    effective(near_begin, mid_begin, chunks, bias_ref)
    far_last_ref[: 3 * CHUNK] = far_own_ref[...]
    pkv_ref[:, :COLS], pkv_ref[:, COLS:] = pk_ref[...], pv_ref[...]
    prev_bias = jnp.where(near_begin < place()[0], 0.0, NEGATIVE)
    for h in range(HEADS_DEV):
        cols = head_cols(h)[0]
        top, sums, out = level(
            h, q_ref[:, cols].T, pkv_ref, False, prev_bias, chunks, bias_ref, s_ref
        )
        top_a = top_ref[h : h + 1, :]
        both = jnp.maximum(top, top_a)
        scale, scale_a = jnp.exp2(top - both), jnp.exp2(top_a - both)
        sums = sums * scale + sums_ref[h : h + 1, :] * scale_a
        out = out * scale + out_ref[cols, :] * scale_a
        att_ref[:, cols] = (out / sums).T.astype(bf16)
        lse_ref[h : h + 1, :] = both + jnp.log2(sums)
    me = lax.axis_index("head")
    zl, x = me >> 2, me & 3

    def projected(dx, dz):
        columns = weight_cols(zl, x, dx, dz)[1]
        return dot(att_ref[...], w_ref[:, columns], 1, 0).astype(bf16)

    behind[:BLOCK], behind[BLOCK:] = projected(1, 1), projected(2, 0)
    ahead[:BLOCK], ahead[BLOCK:] = projected(3, 0), projected(2, 1)
    late_behind[...], late_ahead[...] = projected(1, 0), projected(3, 1)
    own[:BLOCK], own[BLOCK:] = projected(0, 0), projected(0, 1)


def step(keys, values, q, do, q_t, do_t, delta, exponents):
    w = jnp.exp2(exponents(dot(keys, q_t, 1, 0)))
    ds = (w * (dot(values, do_t, 1, 0) - delta)).astype(bf16)
    dv = dot(w.astype(bf16), do, 1, 0)
    dk = dot(ds, q, 1, 0) * SCALING
    return dk, dv, dot(keys, ds, 0, 0)


def far_part(first, refs, bias_ref, near_begin, out_ref, dq_in, dq_out):
    q_ref, far_ref, lse_ref, do_ref, delta_ref = refs
    s, z, y, c = place()
    for i in range(Y):
        for dz in range(Z):
            b = block_of(z, y, c, first + behind_y(i), dz)
            bias_ref[i * Z + dz] = jnp.where(b < near_begin, MID_BIAS, NEGATIVE)
    for h in range(HEADS_DEV):
        cols, vcols = head_cols(h)
        q, do = q_ref[:, cols], do_ref[:, cols]
        q_t, do_t = q.T, do.T
        lse, delta = lse_ref[h : h + 1, :], delta_ref[h : h + 1, :]

        def body(i, acc):
            rows = chunk_rows(i)
            dk, dv, dq = step(
                far_ref[rows, cols], far_ref[rows, vcols], q, do, q_t, do_t, delta,
                lambda p: chunk_exponents(bias_ref, i, p, lse),
            )
            target = chunk_rows(behind_y(i))
            out_ref[target, cols] = dk.astype(bf16)
            out_ref[target, vcols] = dv.astype(bf16)
            return acc + dq

        dq_out[cols, :] = lax.fori_loop(0, Y, body, dq_in[cols, :], unroll=2)


def project_kernel(w_ref, att_ref, *refs):
    grads = refs[: X + 1]
    do_ref, delta_ref, own_ref, other_ref = refs[X + 1 :]
    s, z, y, c = place()
    me = lax.axis_index("head")
    zl, x = me >> 2, me & 3
    acc = jnp.zeros((BLOCK, COLS), f32)
    for i in range(ZL * X):
        device, columns = weight_cols(zl, x, i % X, i // X)
        dx, dz = i % X, i // X
        if dx == 2:
            grad = grads[2 + dz][...]
        else:
            grad = grads[dx + dx // 3][dz * BLOCK : (dz + 1) * BLOCK]
        acc = acc + dot(grad, w_ref[:, columns], 1, 1)
        term = dot(grad, att_ref[...], 0, 0).astype(bf16)
        for part in range(COLS // MIDS):
            block = device * (COLS // MIDS) + part
            bz, by = block >> 3, (block >> 1) & 3
            row = pl.multiple_of((((y - by) & 3) * Z + ((z - bz) & 3)) * MIDS, MIDS)
            piece = term[part * MIDS : (part + 1) * MIDS]

            @pl.when(c == part % 2)
            def _():
                own_ref[pl.ds(row, MIDS), :] = piece

            @pl.when(c != part % 2)
            def _():
                other_ref[pl.ds(row, MIDS), :] = piece

    do_ref[...] = acc.astype(bf16)
    for h in range(HEADS_DEV):
        cols, _ = head_cols(h)
        product = do_ref[:, cols].astype(f32) * att_ref[:, cols].astype(f32)
        delta_ref[h : h + 1, :] = jnp.sum(product.T, axis=0, keepdims=True)


def far_kernel(
    first, nw_hbm, q_ref, far_ref, lse_ref, do_ref, delta_ref, dq_in, weight_ref, out_ref, dq_ref,
    nw_ref, bias_ref, sems,
):
    copy = pltpu.make_async_copy(nw_hbm, nw_ref, sems.at[0])
    copy.start()
    out_ref[:, 2 * COLS :] = weight_ref[...]
    copy.wait()
    s = place()[0]
    near_begin = jnp.maximum(s + 1 - nw_ref[s], 0)
    parts = (q_ref, far_ref, lse_ref, do_ref, delta_ref)
    far_part(first, parts, bias_ref, near_begin, out_ref, dq_in, dq_ref)


def prev_kernel(
    nw_hbm, q_ref, pkv_ref, lse_ref, do_ref, delta_ref, rim_ref, dq_ref, nw_ref, sems
):
    copy = pltpu.make_async_copy(nw_hbm, nw_ref, sems.at[0])
    copy.start()
    copy.wait()
    s = place()[0]
    near_begin = jnp.maximum(s + 1 - nw_ref[s], 0)
    prev_bias = jnp.where(near_begin < s, 0.0, NEGATIVE)
    for h in range(HEADS_DEV):
        cols, vcols = head_cols(h)
        q, do = q_ref[:, cols], do_ref[:, cols]
        q_t, do_t = q.T, do.T
        lse, delta = lse_ref[h : h + 1, :], delta_ref[h : h + 1, :]
        acc = jnp.zeros((HEAD_DIM, BLOCK), f32)
        for part in range(2):
            rows = slice(part * HALF, (part + 1) * HALF)
            dk, dv, dq = step(
                pkv_ref[rows, cols], pkv_ref[rows, vcols], q, do, q_t, do_t, delta,
                lambda p: p * SCORE_SCALE + (prev_bias - lse),
            )
            rim_ref[rows, cols] = dk.astype(bf16)
            rim_ref[rows, vcols] = dv.astype(bf16)
            acc = acc + dq
        dq_ref[cols, :] = acc


def near_kernel(q_ref, kv_ref, lse_ref, do_ref, delta_ref, dq_in, dq_ref, near_ref):
    for h in range(HEADS_DEV):
        cols, vcols = head_cols(h)
        q, do = q_ref[:, cols], do_ref[:, cols]
        q_t, do_t = q.T, do.T
        lse, delta = lse_ref[h : h + 1, :], delta_ref[h : h + 1, :]
        acc = dq_in[cols, :]
        for part in range(2):
            rows = slice(part * HALF, (part + 1) * HALF)
            dk, dv, dq = step(
                kv_ref[rows, cols], kv_ref[rows, vcols], q, do, q_t, do_t, delta,
                lambda p: jnp.where(own_mask(part * HALF), p * SCORE_SCALE - lse, NEGATIVE),
            )
            near_ref[rows, cols] = dk
            near_ref[rows, vcols] = dv
            acc = acc + dq
        dq_ref[:, cols] = (acc * SCALING).T.astype(bf16)


def core_kernel(own_ref, got_ref, *outs):
    def chunk(i):
        rows = slice(i * CHUNK, (i + 1) * CHUNK)
        return (wide(own_ref, rows) + wide(got_ref, rows)).astype(bf16)

    emit(chunk, outs)


def y_kernel(*refs):
    a, b = halves(*refs[:5])
    both = [h[i * MIDS : (i + 1) * MIDS] for h in (a, b) for i in range(2)]
    for out, chunk in zip(refs[5:], both):
        out[...] = chunk.astype(out.dtype)


def total(refs, rows):
    return sum((wide(ref, rows) for ref in refs[1:]), wide(refs[0], rows))


def x_kernel(own, got_behind, got_ahead, last_behind, last_ahead, keep_ref, pass_ref):
    a, b = halves(own, got_behind, got_ahead, last_behind, last_ahead)
    keep_ref[...] = a
    pass_ref[...] = b.astype(bf16)


def pair_kernel(keep_ref, got_ref, out_ref):
    out_ref[...] = (keep_ref[...] + got_ref[...].astype(f32)).astype(bf16)


def last_kernel(*refs):
    near_ref, rim_ref, key_ref, value_ref, weight_ref = refs[Z:]
    sums = total(refs[:Z], slice(0, MIDS))
    weight_ref[...] = sums[:, 2 * COLS :]
    mid = sums[:, : 2 * COLS] * (1.0 / POOL_MID)
    spread = jnp.broadcast_to(mid[:, None, :], (MIDS, POOL_MID, 2 * COLS)).reshape(BLOCK, 2 * COLS)
    grad = near_ref[...] + rim_ref[...].astype(f32) + spread
    key_ref[...] = grad[:, :COLS].astype(bf16)
    value_ref[...] = grad[:, COLS:].astype(bf16)


def on_device(queries, key_frames, value_frames, out_weight, out_grad, near_window, mid_start):
    dma = pltpu.SemaphoreType.DMA
    smem_window = pltpu.SMEM((Z * Y * C,), jnp.int32)
    smem_bias = pltpu.SMEM(((Y + 1) * Z,), f32)
    vmem_scores = pltpu.VMEM((BLOCK + (Y + 1) * CHUNK, BLOCK), f32)
    grad_t = shape(COLS, BLOCK, dtype=f32)
    rows_t = shape(HEADS_DEV, BLOCK, dtype=f32)
    half_rows = FAR_KEYS // 2
    pair_flops = 2 * HEADS_DEV * BLOCK * HEAD_DIM

    kv = jnp.concatenate([key_frames, value_frames], axis=1)
    (mid,) = call(pool_kernel, [shape(MIDS, 2 * COLS)])(kv)
    pair = along_head(out_grad, dz=1)
    run, grads = call(gather_kernel, [shape(CHUNK, 2 * COLS), shape(2 * BLOCK, COLS)])(
        mid, *[along_z(mid, i) for i in range(1, Z)], out_grad, pair
    )
    ahead, behind = along_y(run, 1), along_y(run, -1)
    ahead_g, behind_g = along_x(grads, 1), along_x(grads, -1)
    first, rest, three, keys = call(
        part_kernel,
        [shape(CHUNK // 2, 2 * COLS)] * 2 + [shape(3 * CHUNK, 2 * COLS), shape(BLOCK, COLS)],
    )(run, ahead, behind, kv)
    prev_keys, prev_values = passed_along(keys, 1), passed_along(value_frames, 1)
    three_other = along_seq(three, dc=1)
    scratch = [vmem_scores, smem_window, smem_window, smem_bias, dma((2,))]
    far_three, top, sums, out = call(
        first_kernel,
        [shape(3 * CHUNK, 2 * COLS), rows_t, rows_t, grad_t],
        scratch,
        far=2,
        flops=4 * pair_flops * 1536,
        count=2 * BLOCK * 1536,
    )(near_window, mid_start, queries, kv, three)
    last, *beyond = call(
        join_kernel,
        [shape(CHUNK, 2 * COLS), shape(BLOCK, COLS), shape(BLOCK, COLS)],
        after=(prev_keys, top),
    )(along_y(first, 1), along_y(rest, -1), ahead_g, behind_g)
    last_other = along_seq(last, dc=1)
    grads = [grads, ahead_g, along_x(beyond[0], 1), along_x(beyond[1], -1), behind_g]

    far_own, far_other, prev_kv, attention, lse, *parts = call(
        second_kernel,
        [
            shape(half_rows, 2 * COLS),
            shape(half_rows, 2 * COLS),
            shape(BLOCK, 2 * COLS),
            shape(BLOCK, COLS),
            rows_t,
            *ring_shapes(2 * BLOCK, COLS),
        ],
        scratch,
        far=2,
        flops=4 * pair_flops * 1536 + 2 * BLOCK * 2048 * COLS,
        count=2 * BLOCK * 1536,
    )(
        near_window, mid_start, queries, out_weight, prev_keys, prev_values, last, three_other,
        last_other, far_three, top, sums, out,
    )

    attention_grad, delta, weight_own, weight_other = call(
        project_kernel,
        [shape(BLOCK, COLS), rows_t, shape(half_rows, COLS), shape(half_rows, COLS)],
        flops=4 * BLOCK * 2048 * COLS,
    )(out_weight, attention, *grads)
    rim, dq = call(
        prev_kernel,
        [shape(BLOCK, 2 * COLS), grad_t],
        [smem_window, dma((1,))],
        far=1,
        flops=10 * pair_flops * 512,
        count=2 * BLOCK * 512,
    )(near_window, queries, prev_kv, lse, attention_grad, delta)
    rim_got = passed_along(rim, -1)

    def far_grads(first, far, weight, dq):
        return call(
            functools.partial(far_kernel, first),
            [shape(half_rows, SUM_COLS), grad_t],
            [smem_window, smem_bias, dma((1,))],
            far=1,
            flops=10 * pair_flops * 1024,
            count=2 * BLOCK * 1024,
        )(near_window, queries, far, lse, attention_grad, delta, dq, weight)

    sums_other, dq = far_grads(Y, far_other, weight_other, dq)
    sums_got = along_seq(sums_other, dc=1)
    sums_own, dq = far_grads(0, far_own, weight_own, dq)
    sums = call(core_kernel, ring_shapes(CHUNK, SUM_COLS))(sums_own, sums_got)
    query_grad, near_grad = call(
        near_kernel,
        [shape(BLOCK, COLS), shape(BLOCK, 2 * COLS, dtype=f32)],
        flops=10 * pair_flops * 512,
        count=2 * BLOCK * 512,
        after=(sums[0], rim_got),
    )(queries, kv, lse, attention_grad, delta, dq)

    parts, _ = ring(parts, along_x, after=(near_grad,))
    sums, turned = ring(sums, along_y, after=(near_grad,))
    keep, given = call(
        x_kernel, [shape(BLOCK, COLS, dtype=f32), shape(BLOCK, COLS)], after=(turned,)
    )(*parts)
    given = along_head(given, dz=1)
    sums = call(y_kernel, [shape(MIDS, SUM_COLS, dtype=f32)] + [shape(MIDS, SUM_COLS)] * 3)(*sums)
    sums = [sums[0]] + [along_z(sums[i], -i) for i in range(1, Z)]
    (layer_out,) = call(pair_kernel, [shape(BLOCK, COLS)])(keep, given)
    key_grad, value_grad, weight_t = call(
        last_kernel,
        [shape(BLOCK, COLS), shape(BLOCK, COLS), shape(MIDS, COLS, dtype=f32)],
    )(*sums, near_grad, rim_got)
    return layer_out, query_grad, key_grad, value_grad, weight_t.T


def solution(mesh):
    return jax.shard_map(
        on_device,
        mesh=mesh,
        in_specs=(
            P("seq", "head"),
            P("seq", "head"),
            P("seq", "head"),
            P("head", None),
            P("seq", "head"),
            P(),
            P(),
        ),
        out_specs=(
            P("seq", "head"),
            P("seq", "head"),
            P("seq", "head"),
            P("seq", "head"),
            P("head", "seq"),
        ),
        check_vma=False,
    )
```

```python
import functools
import math

import jax
import jax.numpy as jnp
from jax import lax
from jax.experimental import pallas as pl
from jax.experimental.pallas import tpu as pltpu
from jax.sharding import PartitionSpec as P

HEAD_DIM = 128
BLOCK = 512
POOL_MID = 8
MIDS = BLOCK // POOL_MID
HEADS_DEV = 2
COLS = HEADS_DEV * HEAD_DIM
Z, Y, C = 4, 4, 2
ZL, X = 2, 4
CHUNK = Z * MIDS
CHUNKS = Y * C
FAR_KEYS = CHUNKS * CHUNK
HALF = BLOCK // 2
SUM_COLS = 3 * COLS

NEGATIVE = -1e30
SCALING = HEAD_DIM ** (-0.5)
SCORE_SCALE = SCALING * math.log2(math.e)
MID_BIAS = math.log2(POOL_MID)

bf16 = jnp.bfloat16
f32 = jnp.float32


def along_seq(value, dz=0, dy=0, dc=0):
    pairs = []
    for z in range(Z):
        for y in range(Y):
            for c in range(C):
                target = (((z + dz) % Z) * Y + (y + dy) % Y) * C + (c + dc) % C
                pairs.append(((z * Y + y) * C + c, target))
    return lax.ppermute(value, "seq", pairs)


def along_head(value, dz=0, dx=0):
    pairs = []
    for z in range(ZL):
        for x in range(X):
            pairs.append((z * X + x, ((z + dz) % ZL) * X + (x + dx) % X))
    return lax.ppermute(value, "head", pairs)


def along_z(value, step):
    return along_seq(value, dz=step)


def along_y(value, step):
    return along_seq(value, dy=step)


def along_x(value, step):
    return along_head(value, dx=step)


def passed_along(value, steps):
    count = Z * Y * C
    initial, last = (max(0, -steps), min(count, count - steps))
    return lax.ppermute(value, "seq", [(source, source + steps) for source in range(initial, last)])


def shape(*dims, dtype=bf16):
    return jax.ShapeDtypeStruct(dims, dtype)


def call(kernel, outs, scratch=(), far=0, flops=0, count=0, after=()):
    def run(*args):
        moved = sum(a.size * a.dtype.itemsize for a in (*args, *outs))

        def body(*refs):
            kernel(*refs[: len(args)], *refs[len(args) + len(after) :])

        return pl.pallas_call(
            body,
            out_shape=list(outs),
            in_specs=[pl.BlockSpec(memory_space=pltpu.HBM)] * far
            + [pl.BlockSpec(memory_space=pltpu.VMEM)] * (len(args) - far)
            + [pl.BlockSpec(memory_space=pl.ANY)] * len(after),
            out_specs=[pl.BlockSpec(memory_space=pltpu.VMEM)] * len(outs),
            scratch_shapes=list(scratch),
            cost_estimate=pl.CostEstimate(flops=flops, bytes_accessed=moved, transcendentals=count),
            compiler_params=pltpu.CompilerParams(vmem_limit_bytes=26 * 1024 * 1024),
        )(*args, *after)

    return run


def place():
    s = lax.axis_index("seq")
    return s, s >> 3, (s >> 1) & 3, s & 1


def block_of(z, y, c, group, dz):
    core = (c + (group >> 2)) & 1
    return ((z - dz) & 3) * 8 + ((y - group) & 3) * 2 + core


def behind_y(i):
    return i ^ (i >> 1)


def dot(a, b, da, db):
    return lax.dot_general(a, b, (((da,), (db,)), ((), ())), preferred_element_type=f32)


def wide(ref, rows):
    return ref[rows].astype(f32)


def emit(chunk, outs):
    behind, ahead, late_behind, late_ahead, own = outs
    h = chunk(0).shape[0] // 2
    behind[:h], behind[h:] = chunk(1)[h:], chunk(2)[:h]
    ahead[:h], ahead[h:] = chunk(3)[:h], chunk(2)[h:]
    late_behind[...], late_ahead[...] = chunk(1)[:h], chunk(3)[h:]
    own[...] = chunk(0)


def ring_shapes(rows, width):
    h = rows // 2
    return [shape(rows, width)] * 2 + [shape(h, width)] * 2 + [shape(rows, width)]


def turn_kernel(late_behind, late_ahead, got_behind, got_ahead, out_behind, out_ahead):
    h = late_behind.shape[0]
    rest, all_rows = slice(h, 2 * h), slice(0, h)
    out_behind[...] = (wide(late_behind, all_rows) + wide(got_behind, rest)).astype(bf16)
    out_ahead[...] = (wide(late_ahead, all_rows) + wide(got_ahead, rest)).astype(bf16)


def ring(parts, along, after=()):
    behind, ahead, late_behind, late_ahead, own = parts
    got_behind, got_ahead = along(behind, -1), along(ahead, 1)
    turned = [shape(*late_behind.shape)] * 2
    out_behind, out_ahead = call(turn_kernel, turned, after=after)(
        late_behind, late_ahead, got_behind, got_ahead
    )
    sent = along(out_behind, -1), along(out_ahead, 1)
    return (own, got_behind, got_ahead, *sent), out_behind


def halves(own, got_behind, got_ahead, last_behind, last_ahead):
    h = last_behind.shape[0]
    first, rest = slice(0, h), slice(h, 2 * h)
    a = wide(own, first) + wide(got_ahead, first) + wide(last_behind, first)
    b = wide(own, rest) + wide(got_behind, first) + wide(last_ahead, first)
    return a, b


def pool_kernel(kv_ref, mid_ref):
    row = lax.broadcasted_iota(jnp.int32, (MIDS, BLOCK), 0)
    col = lax.broadcasted_iota(jnp.int32, (MIDS, BLOCK), 1)
    mean = jnp.where(row == col // POOL_MID, 1.0 / POOL_MID, 0.0).astype(bf16)
    mid_ref[...] = dot(mean, kv_ref[...], 1, 0).astype(bf16)


def gather_kernel(mid_ref, a, b, c, grad_ref, pair_ref, run_ref, grads_out):
    for i, ref in enumerate((mid_ref, a, b, c)):
        run_ref[i * MIDS : (i + 1) * MIDS] = ref[...]
    grads_out[:BLOCK] = grad_ref[...]
    grads_out[BLOCK:] = pair_ref[...]


def part_kernel(run_ref, ahead_ref, behind_ref, kv_ref, first_ref, rest_ref, three_ref, keys_out):
    h = CHUNK // 2
    first_ref[...] = ahead_ref[:h]
    rest_ref[...] = behind_ref[h:]
    for i, ref in enumerate((run_ref, ahead_ref, behind_ref)):
        three_ref[i * CHUNK : (i + 1) * CHUNK] = ref[...]
    keys_out[...] = kv_ref[:, :COLS]


def join_kernel(three, first, rest, grads_1, grads_3, mids_ref, own_out, pair_out):
    at = 0
    for ref in (three, first, rest):
        mids_ref[at : at + ref.shape[0]] = ref[...]
        at += ref.shape[0]
    own_out[...] = grads_1[:BLOCK]
    pair_out[...] = grads_3[BLOCK:]


def own_mask(first_key):
    key = lax.broadcasted_iota(jnp.int32, (HALF, BLOCK), 0) + first_key
    query = lax.broadcasted_iota(jnp.int32, (HALF, BLOCK), 1)
    return key <= query


def chunk_exponents(bias_ref, g, product, top):
    return jnp.concatenate(
        [
            product[d * MIDS : (d + 1) * MIDS] * SCORE_SCALE + (bias_ref[g * Z + d] - top)
            for d in range(Z)
        ],
        axis=0,
    )


def chunk_rows(g):
    return pl.ds(pl.multiple_of(g * CHUNK, CHUNK), CHUNK)


def head_cols(h):
    return slice(h * HEAD_DIM, (h + 1) * HEAD_DIM), slice(
        COLS + h * HEAD_DIM, COLS + (h + 1) * HEAD_DIM
    )


def weight_cols(zl, x, dx, dz):
    device = ((zl + dz) & 1) * X + ((x - dx) & 3)
    return device, pl.ds(pl.multiple_of(device * COLS, COLS), COLS)


def effective(near_begin, mid_begin, chunks, bias_ref):
    s, z, y, c = place()
    row = lax.broadcasted_iota(jnp.int32, (CHUNK, CHUNK), 0)
    col = lax.broadcasted_iota(jnp.int32, (CHUNK, CHUNK), 1)
    same = jnp.where(row == col, 1.0, 0.0)
    mean = jnp.where(row // POOL_MID == col // POOL_MID, 1.0 / POOL_MID, 0.0)
    for i, (core, number, mids_ref, mids_row, far_ref, far_row) in enumerate(chunks):
        picks = []
        for dz in range(Z):
            b = block_of(z, y, c, core * Y + behind_y(number), dz)
            bias_ref[i * Z + dz] = jnp.where(b < near_begin, MID_BIAS, NEGATIVE)
            far = jnp.where(b < mid_begin, 1.0, 0.0)
            rows = slice(dz * MIDS, (dz + 1) * MIDS)
            picks.append(same[rows] + far * (mean[rows] - same[rows]))
        pick = jnp.concatenate(picks, axis=0).astype(bf16)
        mids = mids_ref[mids_row : mids_row + CHUNK, :]
        far_ref[far_row : far_row + CHUNK, :] = dot(pick, mids, 1, 0).astype(bf16)


def window(nw_hbm, ms_hbm, nw_ref, ms_ref, sems):
    copies = [
        pltpu.make_async_copy(a, b, sems.at[i])
        for i, (a, b) in enumerate(((nw_hbm, nw_ref), (ms_hbm, ms_ref)))
    ]
    for copy in copies:
        copy.start()
    for copy in copies:
        copy.wait()
    s = place()[0]
    near_begin = jnp.maximum(s + 1 - nw_ref[s], 0)
    return near_begin, jnp.minimum(ms_ref[s], near_begin)


def level(h, q_t, near_ref, near_mask, near_bias, chunks, bias_ref, s_ref):
    cols, vcols = head_cols(h)
    top = jnp.full((1, BLOCK), 0.1 * NEGATIVE, f32)

    def highest(top, product, bias):
        return jnp.maximum(top, jnp.max(product, axis=0, keepdims=True) * SCORE_SCALE + bias)

    for part in range(2):
        rows = slice(part * HALF, (part + 1) * HALF)
        product = dot(near_ref[rows, cols], q_t, 1, 0)
        if near_mask:
            product = jnp.where(own_mask(part * HALF), product, NEGATIVE)
        s_ref[rows, :] = product
        top = highest(top, product, near_bias)

    for g, (_, _, _, _, far_ref, row) in enumerate(chunks):
        product = dot(far_ref[row : row + CHUNK, cols], q_t, 1, 0)
        s_ref[BLOCK + g * CHUNK : BLOCK + (g + 1) * CHUNK, :] = product
        for d in range(Z):
            top = highest(top, product[d * MIDS : (d + 1) * MIDS], bias_ref[g * Z + d])

    def values_of(exponents, values):
        e = jnp.exp2(exponents)
        return jnp.sum(e, axis=0, keepdims=True), dot(values, e.astype(bf16), 0, 0)

    sums, out = jnp.zeros((1, BLOCK), f32), jnp.zeros((HEAD_DIM, BLOCK), f32)
    for g, (_, _, _, _, far_ref, row) in enumerate(chunks):
        product = s_ref[BLOCK + g * CHUNK : BLOCK + (g + 1) * CHUNK, :]
        exponents = chunk_exponents(bias_ref, g, product, top)
        a, b = values_of(exponents, far_ref[row : row + CHUNK, vcols])
        sums, out = sums + a, out + b
    for part in range(2):
        rows = slice(part * HALF, (part + 1) * HALF)
        a, b = values_of(s_ref[rows, :] * SCORE_SCALE + (near_bias - top), near_ref[rows, vcols])
        sums, out = sums + a, out + b
    return top, sums, out


def first_kernel(
    nw_hbm, ms_hbm, q_ref, kv_ref, mids_ref, far_ref, top_ref, sums_ref, out_ref,
    s_ref, nw_ref, ms_ref, bias_ref, sems,
):
    near_begin, mid_begin = window(nw_hbm, ms_hbm, nw_ref, ms_ref, sems)
    chunks = [(0, i, mids_ref, i * CHUNK, far_ref, i * CHUNK) for i in range(3)]
    effective(near_begin, mid_begin, chunks, bias_ref)
    for h in range(HEADS_DEV):
        top, sums, out = level(
            h, q_ref[:, head_cols(h)[0]].T, kv_ref, True, 0.0, chunks, bias_ref, s_ref
        )
        top_ref[h : h + 1, :] = top
        sums_ref[h : h + 1, :] = sums
        out_ref[head_cols(h)[0], :] = out


def second_kernel(
    nw_hbm, ms_hbm, q_ref, w_ref, pk_ref, pv_ref, mids_ref, other_ref, far_own_ref,
    top_ref, sums_ref, out_ref, far_last_ref, far_ref, pkv_ref, att_ref, lse_ref, behind, ahead, late_behind, late_ahead, own,
    s_ref, nw_ref, ms_ref, bias_ref, sems,
):
    near_begin, mid_begin = window(nw_hbm, ms_hbm, nw_ref, ms_ref, sems)
    chunks = [(0, 3, mids_ref, 3 * CHUNK, far_last_ref, 3 * CHUNK)]
    chunks += [(1, i, other_ref, i * CHUNK, far_ref, i * CHUNK) for i in range(Y)]
    effective(near_begin, mid_begin, chunks, bias_ref)
    far_last_ref[: 3 * CHUNK] = far_own_ref[...]
    pkv_ref[:, :COLS], pkv_ref[:, COLS:] = pk_ref[...], pv_ref[...]
    prev_bias = jnp.where(near_begin < place()[0], 0.0, NEGATIVE)
    for h in range(HEADS_DEV):
        cols = head_cols(h)[0]
        top, sums, out = level(
            h, q_ref[:, cols].T, pkv_ref, False, prev_bias, chunks, bias_ref, s_ref
        )
        top_a = top_ref[h : h + 1, :]
        both = jnp.maximum(top, top_a)
        scale, scale_a = jnp.exp2(top - both), jnp.exp2(top_a - both)
        sums = sums * scale + sums_ref[h : h + 1, :] * scale_a
        out = out * scale + out_ref[cols, :] * scale_a
        att_ref[:, cols] = (out / sums).T.astype(bf16)
        lse_ref[h : h + 1, :] = both + jnp.log2(sums)
    me = lax.axis_index("head")
    zl, x = me >> 2, me & 3

    def projected(dx, dz):
        columns = weight_cols(zl, x, dx, dz)[1]
        return dot(att_ref[...], w_ref[:, columns], 1, 0).astype(bf16)

    behind[:BLOCK], behind[BLOCK:] = projected(1, 1), projected(2, 0)
    ahead[:BLOCK], ahead[BLOCK:] = projected(3, 0), projected(2, 1)
    late_behind[...], late_ahead[...] = projected(1, 0), projected(3, 1)
    own[:BLOCK], own[BLOCK:] = projected(0, 0), projected(0, 1)


def step(keys, values, q, do, q_t, do_t, delta, exponents):
    w = jnp.exp2(exponents(dot(keys, q_t, 1, 0)))
    ds = (w * (dot(values, do_t, 1, 0) - delta)).astype(bf16)
    dv = dot(w.astype(bf16), do, 1, 0)
    dk = dot(ds, q, 1, 0) * SCALING
    return dk, dv, dot(keys, ds, 0, 0)


def far_part(first, refs, bias_ref, near_begin, out_ref, dq_in, dq_out):
    q_ref, far_ref, lse_ref, do_ref, delta_ref = refs
    s, z, y, c = place()
    for i in range(Y):
        for dz in range(Z):
            b = block_of(z, y, c, first + behind_y(i), dz)
            bias_ref[i * Z + dz] = jnp.where(b < near_begin, MID_BIAS, NEGATIVE)
    for h in range(HEADS_DEV):
        cols, vcols = head_cols(h)
        q, do = q_ref[:, cols], do_ref[:, cols]
        q_t, do_t = q.T, do.T
        lse, delta = lse_ref[h : h + 1, :], delta_ref[h : h + 1, :]

        def body(i, acc):
            rows = chunk_rows(i)
            dk, dv, dq = step(
                far_ref[rows, cols], far_ref[rows, vcols], q, do, q_t, do_t, delta,
                lambda p: chunk_exponents(bias_ref, i, p, lse),
            )
            target = chunk_rows(behind_y(i))
            out_ref[target, cols] = dk.astype(bf16)
            out_ref[target, vcols] = dv.astype(bf16)
            return acc + dq

        dq_out[cols, :] = lax.fori_loop(0, Y, body, dq_in[cols, :], unroll=2)


def project_kernel(w_ref, att_ref, *refs):
    grads = refs[: X + 1]
    do_ref, delta_ref, own_ref, other_ref = refs[X + 1 :]
    s, z, y, c = place()
    me = lax.axis_index("head")
    zl, x = me >> 2, me & 3
    acc = jnp.zeros((BLOCK, COLS), f32)
    for i in range(ZL * X):
        device, columns = weight_cols(zl, x, i % X, i // X)
        dx, dz = i % X, i // X
        if dx == 2:
            grad = grads[2 + dz][...]
        else:
            grad = grads[dx + dx // 3][dz * BLOCK : (dz + 1) * BLOCK]
        acc = acc + dot(grad, w_ref[:, columns], 1, 1)
        term = dot(grad, att_ref[...], 0, 0).astype(bf16)
        for part in range(COLS // MIDS):
            block = device * (COLS // MIDS) + part
            bz, by = block >> 3, (block >> 1) & 3
            row = pl.multiple_of((((y - by) & 3) * Z + ((z - bz) & 3)) * MIDS, MIDS)
            piece = term[part * MIDS : (part + 1) * MIDS]

            @pl.when(c == part % 2)
            def _():
                own_ref[pl.ds(row, MIDS), :] = piece

            @pl.when(c != part % 2)
            def _():
                other_ref[pl.ds(row, MIDS), :] = piece

    do_ref[...] = acc.astype(bf16)
    for h in range(HEADS_DEV):
        cols, _ = head_cols(h)
        product = do_ref[:, cols].astype(f32) * att_ref[:, cols].astype(f32)
        delta_ref[h : h + 1, :] = jnp.sum(product.T, axis=0, keepdims=True)


def far_kernel(
    first, nw_hbm, q_ref, far_ref, lse_ref, do_ref, delta_ref, dq_in, weight_ref, out_ref, dq_ref,
    nw_ref, bias_ref, sems,
):
    copy = pltpu.make_async_copy(nw_hbm, nw_ref, sems.at[0])
    copy.start()
    out_ref[:, 2 * COLS :] = weight_ref[...]
    copy.wait()
    s = place()[0]
    near_begin = jnp.maximum(s + 1 - nw_ref[s], 0)
    parts = (q_ref, far_ref, lse_ref, do_ref, delta_ref)
    far_part(first, parts, bias_ref, near_begin, out_ref, dq_in, dq_ref)


def prev_kernel(
    nw_hbm, q_ref, pkv_ref, lse_ref, do_ref, delta_ref, rim_ref, dq_ref, nw_ref, sems
):
    copy = pltpu.make_async_copy(nw_hbm, nw_ref, sems.at[0])
    copy.start()
    copy.wait()
    s = place()[0]
    near_begin = jnp.maximum(s + 1 - nw_ref[s], 0)
    prev_bias = jnp.where(near_begin < s, 0.0, NEGATIVE)
    for h in range(HEADS_DEV):
        cols, vcols = head_cols(h)
        q, do = q_ref[:, cols], do_ref[:, cols]
        q_t, do_t = q.T, do.T
        lse, delta = lse_ref[h : h + 1, :], delta_ref[h : h + 1, :]
        acc = jnp.zeros((HEAD_DIM, BLOCK), f32)
        for part in range(2):
            rows = slice(part * HALF, (part + 1) * HALF)
            dk, dv, dq = step(
                pkv_ref[rows, cols], pkv_ref[rows, vcols], q, do, q_t, do_t, delta,
                lambda p: p * SCORE_SCALE + (prev_bias - lse),
            )
            rim_ref[rows, cols] = dk.astype(bf16)
            rim_ref[rows, vcols] = dv.astype(bf16)
            acc = acc + dq
        dq_ref[cols, :] = acc


def near_kernel(q_ref, kv_ref, lse_ref, do_ref, delta_ref, dq_in, dq_ref, near_ref):
    for h in range(HEADS_DEV):
        cols, vcols = head_cols(h)
        q, do = q_ref[:, cols], do_ref[:, cols]
        q_t, do_t = q.T, do.T
        lse, delta = lse_ref[h : h + 1, :], delta_ref[h : h + 1, :]
        acc = dq_in[cols, :]
        for part in range(2):
            rows = slice(part * HALF, (part + 1) * HALF)
            dk, dv, dq = step(
                kv_ref[rows, cols], kv_ref[rows, vcols], q, do, q_t, do_t, delta,
                lambda p: jnp.where(own_mask(part * HALF), p * SCORE_SCALE - lse, NEGATIVE),
            )
            near_ref[rows, cols] = dk
            near_ref[rows, vcols] = dv
            acc = acc + dq
        dq_ref[:, cols] = (acc * SCALING).T.astype(bf16)


def core_kernel(own_ref, got_ref, *outs):
    def chunk(i):
        rows = slice(i * CHUNK, (i + 1) * CHUNK)
        return (wide(own_ref, rows) + wide(got_ref, rows)).astype(bf16)

    emit(chunk, outs)


def y_kernel(*refs):
    a, b = halves(*refs[:5])
    both = [h[i * MIDS : (i + 1) * MIDS] for h in (a, b) for i in range(2)]
    for out, chunk in zip(refs[5:], both):
        out[...] = chunk.astype(out.dtype)


def total(refs, rows):
    return sum((wide(ref, rows) for ref in refs[1:]), wide(refs[0], rows))


def x_kernel(own, got_behind, got_ahead, last_behind, last_ahead, keep_ref, pass_ref):
    a, b = halves(own, got_behind, got_ahead, last_behind, last_ahead)
    keep_ref[...] = a
    pass_ref[...] = b.astype(bf16)


def pair_kernel(keep_ref, got_ref, out_ref):
    out_ref[...] = (keep_ref[...] + got_ref[...].astype(f32)).astype(bf16)


def last_kernel(*refs):
    near_ref, rim_ref, key_ref, value_ref, weight_ref = refs[Z:]
    sums = total(refs[:Z], slice(0, MIDS))
    weight_ref[...] = sums[:, 2 * COLS :]
    mid = sums[:, : 2 * COLS] * (1.0 / POOL_MID)
    spread = jnp.broadcast_to(mid[:, None, :], (MIDS, POOL_MID, 2 * COLS)).reshape(BLOCK, 2 * COLS)
    grad = near_ref[...] + rim_ref[...].astype(f32) + spread
    key_ref[...] = grad[:, :COLS].astype(bf16)
    value_ref[...] = grad[:, COLS:].astype(bf16)


def on_device(queries, key_frames, value_frames, out_weight, out_grad, near_window, mid_start):
    dma = pltpu.SemaphoreType.DMA
    smem_window = pltpu.SMEM((Z * Y * C,), jnp.int32)
    smem_bias = pltpu.SMEM(((Y + 1) * Z,), f32)
    vmem_scores = pltpu.VMEM((BLOCK + (Y + 1) * CHUNK, BLOCK), f32)
    grad_t = shape(COLS, BLOCK, dtype=f32)
    rows_t = shape(HEADS_DEV, BLOCK, dtype=f32)
    half_rows = FAR_KEYS // 2
    pair_flops = 2 * HEADS_DEV * BLOCK * HEAD_DIM

    kv = jnp.concatenate([key_frames, value_frames], axis=1)
    (mid,) = call(pool_kernel, [shape(MIDS, 2 * COLS)])(kv)
    pair = along_head(out_grad, dz=1)
    run, grads = call(gather_kernel, [shape(CHUNK, 2 * COLS), shape(2 * BLOCK, COLS)])(
        mid, *[along_z(mid, i) for i in range(1, Z)], out_grad, pair
    )
    ahead, behind = along_y(run, 1), along_y(run, -1)
    ahead_g, behind_g = along_x(grads, 1), along_x(grads, -1)
    first, rest, three, keys = call(
        part_kernel,
        [shape(CHUNK // 2, 2 * COLS)] * 2 + [shape(3 * CHUNK, 2 * COLS), shape(BLOCK, COLS)],
    )(run, ahead, behind, kv)
    prev_keys, prev_values = passed_along(keys, 1), passed_along(value_frames, 1)
    scratch = [vmem_scores, smem_window, smem_window, smem_bias, dma((2,))]
    far_three, top, sums, out = call(
        first_kernel,
        [shape(3 * CHUNK, 2 * COLS), rows_t, rows_t, grad_t],
        scratch,
        far=2,
        flops=4 * pair_flops * 1536,
        count=2 * BLOCK * 1536,
    )(near_window, mid_start, queries, kv, three)
    mids_own, *beyond = call(
        join_kernel,
        [shape(half_rows, 2 * COLS), shape(BLOCK, COLS), shape(BLOCK, COLS)],
        after=(prev_keys, top),
    )(three, along_y(first, 1), along_y(rest, -1), ahead_g, behind_g)
    mids_other = along_seq(mids_own, dc=1)
    grads = [grads, ahead_g, along_x(beyond[0], 1), along_x(beyond[1], -1), behind_g]

    far_own, far_other, prev_kv, attention, lse, *parts = call(
        second_kernel,
        [
            shape(half_rows, 2 * COLS),
            shape(half_rows, 2 * COLS),
            shape(BLOCK, 2 * COLS),
            shape(BLOCK, COLS),
            rows_t,
            *ring_shapes(2 * BLOCK, COLS),
        ],
        scratch,
        far=2,
        flops=4 * pair_flops * 1536 + 2 * BLOCK * 2048 * COLS,
        count=2 * BLOCK * 1536,
    )(
        near_window, mid_start, queries, out_weight, prev_keys, prev_values, mids_own, mids_other,
        far_three, top, sums, out,
    )

    attention_grad, delta, weight_own, weight_other = call(
        project_kernel,
        [shape(BLOCK, COLS), rows_t, shape(half_rows, COLS), shape(half_rows, COLS)],
        flops=4 * BLOCK * 2048 * COLS,
    )(out_weight, attention, *grads)
    rim, dq = call(
        prev_kernel,
        [shape(BLOCK, 2 * COLS), grad_t],
        [smem_window, dma((1,))],
        far=1,
        flops=10 * pair_flops * 512,
        count=2 * BLOCK * 512,
    )(near_window, queries, prev_kv, lse, attention_grad, delta)
    rim_got = passed_along(rim, -1)

    def far_grads(first, far, weight, dq):
        return call(
            functools.partial(far_kernel, first),
            [shape(half_rows, SUM_COLS), grad_t],
            [smem_window, smem_bias, dma((1,))],
            far=1,
            flops=10 * pair_flops * 1024,
            count=2 * BLOCK * 1024,
        )(near_window, queries, far, lse, attention_grad, delta, dq, weight)

    sums_other, dq = far_grads(Y, far_other, weight_other, dq)
    sums_got = along_seq(sums_other, dc=1)
    sums_own, dq = far_grads(0, far_own, weight_own, dq)
    sums = call(core_kernel, ring_shapes(CHUNK, SUM_COLS))(sums_own, sums_got)
    query_grad, near_grad = call(
        near_kernel,
        [shape(BLOCK, COLS), shape(BLOCK, 2 * COLS, dtype=f32)],
        flops=10 * pair_flops * 512,
        count=2 * BLOCK * 512,
        after=(sums[0], rim_got),
    )(queries, kv, lse, attention_grad, delta, dq)

    parts, _ = ring(parts, along_x, after=(near_grad,))
    sums, turned = ring(sums, along_y, after=(near_grad,))
    keep, given = call(
        x_kernel, [shape(BLOCK, COLS, dtype=f32), shape(BLOCK, COLS)], after=(turned,)
    )(*parts)
    given = along_head(given, dz=1)
    sums = call(y_kernel, [shape(MIDS, SUM_COLS, dtype=f32)] + [shape(MIDS, SUM_COLS)] * 3)(*sums)
    sums = [sums[0]] + [along_z(sums[i], -i) for i in range(1, Z)]
    (layer_out,) = call(pair_kernel, [shape(BLOCK, COLS)])(keep, given)
    key_grad, value_grad, weight_t = call(
        last_kernel,
        [shape(BLOCK, COLS), shape(BLOCK, COLS), shape(MIDS, COLS, dtype=f32)],
    )(*sums, near_grad, rim_got)
    return layer_out, query_grad, key_grad, value_grad, weight_t.T


def solution(mesh):
    return jax.shard_map(
        on_device,
        mesh=mesh,
        in_specs=(
            P("seq", "head"),
            P("seq", "head"),
            P("seq", "head"),
            P("head", None),
            P("seq", "head"),
            P(),
            P(),
        ),
        out_specs=(
            P("seq", "head"),
            P("seq", "head"),
            P("seq", "head"),
            P("seq", "head"),
            P("head", "seq"),
        ),
        check_vma=False,
    )
```
